128 devices in a mesh: ctx: 16 (over y_hi, z, core), kv: 8 (over x, y_lo).
Axes of the slice: x: 4, y: 4 (y_hi: 2, y_lo: 2; y = y_hi * 2 + y_lo), z: 4, core: 2. Of those that a mesh axis runs over, the one named last changes fastest.
Arguments:
- queries: bfloat16 [2, 512, 128, 128], P(None, 'ctx', 'kv'), may hold values from -6 to 6
- new_keys: bfloat16 [2, 512, 8, 128], P(None, 'ctx', 'kv'), may hold values from -6 to 6
- new_values: bfloat16 [2, 512, 8, 128], P(None, 'ctx', 'kv'), may hold values from -6 to 6
- cache_keys: bfloat16 [2, 32768, 8, 128], P(None, 'ctx', 'kv'), may hold values from -6 to 6
- cache_values: bfloat16 [2, 32768, 8, 128], P(None, 'ctx', 'kv'), may hold values from -6 to 6
- cached_len: int32 [2], replicated, may hold values from 4096 to 32768, as said below
- span_order: int32 [2, 32], replicated, may hold values from 0 to 31, as said below
Outputs:
- attention: bfloat16 [2, 512, 128, 128], P(None, ('ctx', 'kv'))
- log_norm: float32 [2, 512, 128], P(None, ('ctx', 'kv'))
The draws below stay inside these ranges and needn't reach their ends.
Inputs may be any that keep to these rules, and one draw needn't show every extreme that they name: `cached_len`: one request holds all 32768 slots. `span_order`: each row is a permutation in which block slots 2 q and 2 q + 1 hold blocks c and 31 - c for some c.
All inputs are finite; a program needn't handle non-finite values.
Results may differ from the reference program's by a relative error of at most 0.0058.
Values may be sent and summed in bfloat16 or wider, within the bound.
No kernel may reach another device: no remote copies, remote signals or barrier semaphores. Data moves between devices by JAX's collectives and lax.ppermute only.
A program may use at most 64 MiB of HBM per device.

```python
import jax
import jax.numpy as jnp
from jax import lax

HQ = 128
KVH = 8
HD = 128
REQ = 2
CACHE_DEV = 2048
NEW_DEV = 32
CACHE = 32768
NEW = 512
NCHUNK = 32
N_CTX = 16


def draw_queries(key, part):
    key = jax.random.fold_in(key, 11)
    entries = jnp.clip(jax.random.normal(key, (REQ, NEW, HQ, HD), jnp.float32), -4.0, 4.0)
    return entries.astype(jnp.bfloat16)


def draw_cache_keys(key, part):
    key = jax.random.fold_in(key, 12)
    entries = jnp.clip(jax.random.normal(key, (REQ, CACHE, KVH, HD), jnp.float32), -4.0, 4.0)
    return entries.astype(jnp.bfloat16)


def draw_cached_len(key, part):
    key = jax.random.fold_in(key, 13)
    key_one, key_two = jax.random.split(key)
    lengths = jax.random.randint(key_one, (REQ,), CACHE // 8, CACHE + 1)
    full_req = jax.random.randint(key_two, (), 0, REQ)
    return jnp.where(jnp.arange(REQ) == full_req, CACHE, lengths).astype(jnp.int32)


def draw_span_order(key, part):
    key = jax.random.fold_in(key, 14)

    def one_row(row_key):
        key_one, key_two = jax.random.split(row_key)
        rank_of = jax.random.permutation(key_one, N_CTX).astype(jnp.int32)
        pair_of = jnp.zeros((N_CTX,), jnp.int32).at[rank_of].set(jnp.arange(N_CTX, dtype=jnp.int32))
        flipped = jax.random.randint(key_two, (N_CTX,), 0, 2)
        low_span = pair_of
        high_span = NCHUNK - 1 - pair_of
        ordered = jnp.stack([jnp.where(flipped == 1, high_span, low_span), jnp.where(flipped == 1, low_span, high_span)], 1)
        return ordered.reshape(NCHUNK)
    return jax.vmap(one_row)(jax.random.split(key, REQ)).astype(jnp.int32)


def shard_levels(key, dims, cuts, low, largest):
    factor_of = 1.0
    for position, blocks in cuts:
        draws = jax.random.uniform(jax.random.fold_in(jax.random.fold_in(key, 6), position), (blocks,), jnp.float32, low / len(cuts), largest / len(cuts))
        factor_of = factor_of * jnp.repeat(jnp.exp(draws), dims[position] // blocks).reshape((-1,) + (1,) * (len(dims) - 1 - position))
    return factor_of


def gaussian(key, extent, width, reach, pieces=(), held_as=jnp.bfloat16):
    values = width * jax.random.normal(key, extent, jnp.float32)
    if pieces:
        values = values * shard_levels(key, extent, pieces, -0.22, 0.18)
    return jnp.clip(values, -reach, reach).astype(held_as)


def setup_inputs(seed: int = 0) -> dict:
    arg_keys = jax.random.split(jax.random.key(seed), 8)
    return {
        "queries": draw_queries(jax.random.fold_in(arg_keys[7], 71), 0),
        "new_keys": gaussian(arg_keys[1], (REQ, NEW, KVH, HD), 1.0, 6.0, ((1, 16), (2, 8))),
        "new_values": gaussian(arg_keys[2], (REQ, NEW, KVH, HD), 1.0, 6.0, ((1, 16), (2, 8))),
        "cache_keys": draw_cache_keys(jax.random.fold_in(arg_keys[7], 71), 0),
        "cache_values": gaussian(arg_keys[4], (REQ, CACHE, KVH, HD), 1.0, 6.0, ((1, 16), (2, 8))),
        "cached_len": draw_cached_len(jax.random.fold_in(arg_keys[7], 71), 0),
        "span_order": draw_span_order(jax.random.fold_in(arg_keys[7], 71), 0),
    }


masked_score = -1.0e30


def turn_positions(span_order):
    span_rows = NEW_DEV // 2
    slot_index = jnp.arange(NEW, dtype=jnp.int32)
    return span_order[:, slot_index // span_rows] * span_rows + (slot_index % span_rows)[None, :]


def attend_group(q_group, k_group, v_group, visible):
    scores = jnp.einsum("rtgd,rsd->rgts", q_group.astype(jnp.float32), k_group.astype(jnp.float32)) * (HD ** -0.5)
    scores = jnp.where(visible[:, None], scores, masked_score)
    highest = jnp.max(scores, -1, keepdims=True)
    exponent = jnp.exp(scores - highest)
    totals = jnp.sum(exponent, -1, keepdims=True)
    log_total = (highest + jnp.log(totals))[..., 0]
    weights = (exponent / totals).astype(jnp.bfloat16)
    outputs = jnp.einsum("rgts,rsd->rtgd", weights.astype(jnp.float32), v_group.astype(jnp.float32))
    outputs = lax.optimization_barrier(outputs.astype(jnp.bfloat16)).astype(jnp.float32)
    return outputs, jnp.transpose(log_total, (0, 2, 1))


def shard_partial(queries, key_rows, value_rows, visible):
    group_size = HQ // KVH

    def one_kv_head(kv_head):
        q_group = lax.dynamic_slice_in_dim(queries, kv_head * group_size, group_size, 2)
        k_group = lax.dynamic_index_in_dim(key_rows, kv_head, 2, keepdims=False)
        v_group = lax.dynamic_index_in_dim(value_rows, kv_head, 2, keepdims=False)
        return attend_group(q_group, k_group, v_group, visible)

    outputs, log_parts = lax.map(one_kv_head, jnp.arange(KVH, dtype=jnp.int32))
    outputs = jnp.transpose(outputs, (1, 2, 0, 3, 4)).reshape(REQ, NEW, HQ, HD)
    log_parts = jnp.transpose(log_parts, (1, 2, 0, 3)).reshape(REQ, NEW, HQ)
    return outputs, log_parts


def reference(queries, new_keys, new_values, cache_keys, cache_values, cached_len, span_order):
    positions = turn_positions(span_order)

    def cycle_step(running, shard_index):
        highest, totals, summed = running
        key_rows = jnp.concatenate([lax.dynamic_slice_in_dim(cache_keys, shard_index * CACHE_DEV, CACHE_DEV, 1),
                                    lax.dynamic_slice_in_dim(new_keys, shard_index * NEW_DEV, NEW_DEV, 1)], 1)
        value_rows = jnp.concatenate([lax.dynamic_slice_in_dim(cache_values, shard_index * CACHE_DEV, CACHE_DEV, 1),
                                      lax.dynamic_slice_in_dim(new_values, shard_index * NEW_DEV, NEW_DEV, 1)], 1)
        cache_valid = (shard_index * CACHE_DEV + jnp.arange(CACHE_DEV, dtype=jnp.int32))[None, :] < cached_len[:, None]
        key_positions = lax.dynamic_slice_in_dim(positions, shard_index * NEW_DEV, NEW_DEV, 1)
        visible = jnp.concatenate([jnp.broadcast_to(cache_valid[:, None, :], (REQ, NEW, CACHE_DEV)),
                                   key_positions[:, None, :] <= positions[:, :, None]], 2)
        outputs, log_parts = shard_partial(queries, key_rows, value_rows, visible)
        new_high = jnp.maximum(highest, log_parts)
        rescale = jnp.exp(highest - new_high)
        weight_new = jnp.exp(log_parts - new_high)
        totals = totals * rescale + weight_new
        summed = summed * rescale[..., None] + weight_new[..., None] * outputs
        return (new_high, totals, summed), None

    start = (jnp.full((REQ, NEW, HQ), masked_score, jnp.float32), jnp.zeros((REQ, NEW, HQ), jnp.float32),
             jnp.zeros((REQ, NEW, HQ, HD), jnp.float32))
    (highest, totals, summed), _ = lax.scan(cycle_step, start, jnp.arange(N_CTX, dtype=jnp.int32))
    log_norm = highest + jnp.log(totals)
    attention = (summed / totals[..., None]).astype(jnp.bfloat16)
    return attention, log_norm
```

```python
import functools

import jax
import jax.numpy as jnp
from jax import lax
from jax.experimental import pallas as pl
from jax.experimental.pallas import tpu as pltpu
from jax.sharding import Mesh
from jax.sharding import PartitionSpec as P

LOG2E = 1.4426950408889634
LN2 = 0.6931471805599453
MASKED = -1e30
SUM_LOW = 2.0**-60
SUM_HIGH = 2.0**100
VMEM = 56 << 20


def dot_nt(a, b):
    return lax.dot_general(a, b, (((1,), (1,)), ((), ())), preferred_element_type=jnp.float32)


def prepare_kernel(where_ref, len_ref, vo_ref, vp_ref, no_ref, np_ref, ko_ref, kp_ref, vt_ref, kn_ref):
    r = pl.program_id(0)
    rows = vo_ref.shape[1]
    extra = vt_ref.shape[1] - 128
    me = where_ref[0]
    for part, ref in enumerate((vo_ref, vp_ref)):
        owner = me if part == 0 else me + 1 - 2 * lax.rem(me, 2)
        valid = len_ref[r] - owner * rows
        row_id = lax.broadcasted_iota(jnp.int32, (rows, 128), 0)
        kept = jnp.where(row_id < valid, ref[0].astype(jnp.float32), 0.0).astype(jnp.bfloat16)
        vt_ref[0, :128, part * rows : (part + 1) * rows] = jnp.transpose(kept)
        col_id = lax.broadcasted_iota(jnp.int32, (extra, rows), 1)
        vt_ref[0, 128:, part * rows : (part + 1) * rows] = jnp.where(
            col_id < valid, 1.0, 0.0
        ).astype(jnp.bfloat16)
    new = no_ref.shape[1]
    fresh = jnp.concatenate(
        [no_ref[0], np_ref[0], jnp.zeros((128 - 2 * new, 128), jnp.bfloat16)], 0
    )
    vt_ref[0, :128, 2 * rows :] = jnp.transpose(fresh)
    vt_ref[0, 128:, 2 * rows :] = jnp.ones((extra, 128), jnp.bfloat16)
    kn_ref[0, :new, :] = ko_ref[0]
    kn_ref[0, new:, :] = kp_ref[0]


def prepare(where, cached_len, v_own, v_par, n_own, n_par, k_own, k_par):
    requests, rows, dim = v_own.shape
    new = n_own.shape[1]
    whole = lambda n: pl.BlockSpec((1, n, dim), lambda r, *_: (r, 0, 0))
    return pl.pallas_call(
        prepare_kernel,
        grid_spec=pltpu.PrefetchScalarGridSpec(
            num_scalar_prefetch=2,
            grid=(requests,),
            in_specs=[whole(rows), whole(rows), whole(new), whole(new), whole(new), whole(new)],
            out_specs=[
                pl.BlockSpec((1, 144, 2 * rows + 128), lambda r, *_: (r, 0, 0)),
                whole(2 * new),
            ],
        ),
        out_shape=[
            jax.ShapeDtypeStruct((requests, 144, 2 * rows + 128), jnp.bfloat16),
            jax.ShapeDtypeStruct((requests, 2 * new, dim), jnp.bfloat16),
        ],
        compiler_params=pltpu.CompilerParams(vmem_limit_bytes=VMEM),
        cost_estimate=pl.CostEstimate(flops=10**6, bytes_accessed=4 << 20, transcendentals=0),
    )(where, cached_len, v_own, v_par, n_own, n_par, k_own, k_par)


def attend_kernel(
    request, pairs, where_ref, len_ref, span_ref, *refs
):
    n_blocks = 2 * len(pairs)
    q_refs = refs[:n_blocks]
    ko_ref, kp_ref, kn_ref, vt_ref, out_ref = refs[n_blocks : n_blocks + 5]
    q_buf, acc_ref, top_ref, sems = refs[n_blocks + 5 :]
    step = pl.program_id(0)
    me = where_ref[0]
    core = lax.rem(me, 2)
    chip = me // 2
    rows = ko_ref.shape[1]
    n_new = kn_ref.shape[1]
    block = q_buf.shape[1]
    width = 2 * block

    def fetch(n):
        slot = 2 * (n // 2) + (n % 2 + lax.rem(chip, 2)) % 2
        return pltpu.make_async_copy(q_refs[n].at[request], q_buf.at[slot], sems.at[n // 2])

    @pl.when(step == 0)
    def _():
        for n in range(n_blocks):
            fetch(n).start()

    for n in range(n_blocks):

        @pl.when(step == n // 2)
        def _(n=n):
            fetch(n).wait()

    relative = jnp.int32(pairs[0])
    for n, pair in enumerate(pairs):
        relative = jnp.where(step == n, jnp.int32(pair), relative)
    low_chip = 2 * ((chip // 2) ^ relative)

    q = q_buf[pl.ds(2 * step, 2)].reshape(width, 128)
    scale = LOG2E * 128**-0.5

    def span(shard, half):
        return span_ref[request, 2 * shard + half]

    lane = lax.broadcasted_iota(jnp.int32, (1, width), 1)
    q_span = jnp.zeros((1, width), jnp.int32)
    for n in range(4):
        q_span = jnp.where(
            lane // (block // 2) == n, span(2 * (low_chip + n // 2) + core, n % 2), q_span
        )
    q_pos = q_span * 16 + lax.rem(lane // 16, 16)
    key = lax.broadcasted_iota(jnp.int32, (n_new, 1), 0)
    k_span = jnp.zeros((n_new, 1), jnp.int32)
    first_pos = jnp.int32(1 << 30)
    for n in range(4):
        owner = me if n < 2 else me + 1 - 2 * core
        k_span = jnp.where(key // 16 == n, span(owner, n % 2), k_span)
        first_pos = jnp.minimum(first_pos, span(owner, n % 2) * 16)
    shown = (k_span * 16 + lax.rem(key, 16)) <= q_pos

    def new_scores():
        return jnp.where(shown, dot_nt(kn_ref[0], q) * scale, MASKED)

    def values(p, start, size):
        return jnp.dot(
            vt_ref[0, :, pl.ds(start, size)],
            p.astype(jnp.bfloat16),
            preferred_element_type=jnp.float32,
        )

    acc = values(jnp.exp2(dot_nt(ko_ref[0], q) * scale), 0, rows)
    acc = acc + values(jnp.exp2(dot_nt(kp_ref[0], q) * scale), rows, rows)
    acc = acc + values(jnp.exp2(new_scores()), 2 * rows, n_new)
    acc_ref[...] = acc
    top_ref[...] = jnp.zeros_like(top_ref)

    held = [len_ref[request] - (me if n == 0 else me + 1 - 2 * core) * rows for n in range(2)]
    any_cache = jnp.maximum(held[0], held[1]) > 0
    has_key = (q_pos >= first_pos) | any_cache
    total = acc[128:129, :]
    fine = (total < SUM_HIGH) & ((total > SUM_LOW) | jnp.logical_not(has_key))
    redo = jnp.min(jnp.where(fine, 1, 0)) == 0

    @pl.when(redo)
    def _():
        part = 256

        def highest(ref, valid):
            def body(j, top):
                s = dot_nt(ref[0, pl.ds(j * part, part), :], q) * scale
                row = lax.broadcasted_iota(jnp.int32, (part, width), 0) + j * part
                return jnp.maximum(
                    top, jnp.max(jnp.where(row < valid, s, MASKED), 0, keepdims=True)
                )

            return lambda top: lax.fori_loop(0, rows // part, body, top)

        s_new = new_scores()
        top = jnp.max(s_new, 0, keepdims=True)
        top = highest(ko_ref, held[0])(top)
        top = highest(kp_ref, held[1])(top)
        top_ref[...] = jnp.broadcast_to(top, top_ref.shape)
        acc_ref[...] = values(
            jnp.where(shown, jnp.exp2(jnp.minimum(s_new - top, 0.0)), 0.0), 2 * rows, n_new
        )

        def add(ref, first):
            def body(j, carry):
                s = dot_nt(ref[0, pl.ds(j * part, part), :], q) * scale
                start = pl.multiple_of(first + j * part, part)
                acc_ref[...] += values(jnp.exp2(jnp.minimum(s - top, 0.0)), start, part)
                return carry

            lax.fori_loop(0, rows // part, body, 0)

        add(ko_ref, 0)
        add(kp_ref, rows)

    total = acc_ref[128:129, :]
    some = total > 0.0
    inverse = jnp.where(some, 1.0 / jnp.where(some, total, 1.0), 0.0)
    outputs = jnp.transpose(acc_ref[:128, :] * inverse).astype(jnp.bfloat16)
    log_total = jnp.where(
        some, (top_ref[0:1, :] + jnp.log2(jnp.where(some, total, 1.0))) * LN2, MASKED
    )
    high = log_total.astype(jnp.bfloat16).astype(jnp.float32)
    middle = (log_total - high).astype(jnp.bfloat16).astype(jnp.float32)
    low = log_total - high - middle
    logs = jnp.concatenate(
        [high, middle, low, jnp.zeros((5, width), jnp.float32)], 0
    ).astype(jnp.bfloat16)
    owners = out_ref.shape[1]
    share = block // owners
    out_ref[:, :, :share, :] = outputs.reshape(2, owners, share, 128)
    for n in range(2):
        for owner in range(owners):
            start = n * block + owner * share // 128 * 128
            out_ref[n, owner, share:, :] = logs[:, start : start + 128]


def attend(request, pairs, where, cached_len, span_order, blocks, k_own, k_par, k_new, vt):
    rows = k_own.shape[1]
    n_new = k_new.shape[1]
    block = blocks[0].shape[1]
    owners = 8
    share = block // owners
    steps = len(pairs)

    def out_place(step, where_ref, *_):
        relative = jnp.int32(pairs[0])
        for n, pair in enumerate(pairs):
            relative = jnp.where(step == n, jnp.int32(pair), relative)
        return ((where_ref[0] // 4) ^ relative, 0, 0, 0)

    flops = steps * 2 * block * 2 * rows * 128 * 4
    return pl.pallas_call(
        functools.partial(attend_kernel, request, pairs),
        grid_spec=pltpu.PrefetchScalarGridSpec(
            num_scalar_prefetch=3,
            grid=(steps,),
            in_specs=[pl.BlockSpec(memory_space=pl.ANY)] * (2 * steps)
            + [
                pl.BlockSpec((1, rows, 128), lambda s, *_: (request, 0, 0)),
                pl.BlockSpec((1, rows, 128), lambda s, *_: (request, 0, 0)),
                pl.BlockSpec((1, n_new, 128), lambda s, *_: (request, 0, 0)),
                pl.BlockSpec((1, 144, 2 * rows + 128), lambda s, *_: (request, 0, 0)),
            ],
            out_specs=pl.BlockSpec((2, owners, share + 8, 128), out_place),
            scratch_shapes=[
                pltpu.VMEM((2 * steps, block, 128), jnp.bfloat16),
                pltpu.VMEM((144, 2 * block), jnp.float32),
                pltpu.VMEM((8, 2 * block), jnp.float32),
                pltpu.SemaphoreType.DMA((steps,)),
            ],
        ),
        out_shape=jax.ShapeDtypeStruct((8, owners, share + 8, 128), jnp.bfloat16),
        compiler_params=pltpu.CompilerParams(vmem_limit_bytes=VMEM),
        cost_estimate=pl.CostEstimate(
            flops=flops, bytes_accessed=6 << 20, transcendentals=steps * 2 * block * 2 * rows
        ),
    )(where, cached_len, span_order, *blocks, k_own, k_par, k_new, vt)


def combine_kernel(where_ref, in_ref, *refs):
    out_ref, norm_ref = refs[-2:]
    sources, groups = in_ref.shape[:2]
    share = in_ref.shape[2] - 8
    odd = lax.rem(where_ref[1], 2) == 1
    logs = in_ref[:, :, share:, :].astype(jnp.float32)
    logs = logs[:, :, 0, :] + logs[:, :, 1, :] + logs[:, :, 2, :]
    logs = logs.reshape(sources * groups, 128)
    logs = jnp.where(odd, jnp.concatenate([logs[:, 64:], logs[:, :64]], 1), logs)
    logs = logs.reshape(sources, groups, 128)
    highest = jnp.max(logs, 0)
    weight = jnp.exp(logs - highest[None])
    total = jnp.sum(weight, 0)
    norm_ref[...] = highest + jnp.log(total)
    shares = (weight / total[None]).reshape(sources * groups, 128)
    columns = jnp.transpose(
        jnp.concatenate([shares, jnp.zeros((128 - sources * groups, 128), jnp.float32)], 0)
    )
    tokens = out_ref.shape[1]
    for group in range(groups):
        summed = jnp.zeros((share, 128), jnp.float32)
        for source in range(sources):
            n = source * groups + group
            summed = summed + columns[:share, n : n + 1] * in_ref[
                source, group, :share, :
            ].astype(jnp.float32)
        out_ref[0, :, group] = summed.reshape(tokens, share // tokens, 128).astype(jnp.bfloat16)


def combine(request, requests, where, parts, earlier):
    sources, groups, rows, dim = parts.shape
    share = rows - 8
    tokens = share // 16
    shape = (requests, tokens, groups, 16, dim)
    operands = [where, parts] + ([] if earlier is None else [earlier])
    return pl.pallas_call(
        combine_kernel,
        grid_spec=pltpu.PrefetchScalarGridSpec(
            num_scalar_prefetch=1,
            grid=(1,),
            in_specs=[pl.BlockSpec(parts.shape, lambda *_: (0, 0, 0, 0))]
            + ([] if earlier is None else [pl.BlockSpec(memory_space=pl.ANY)]),
            out_specs=[
                pl.BlockSpec((1,) + shape[1:], lambda *_: (request, 0, 0, 0, 0)),
                pl.BlockSpec((groups, 128), lambda *_: (0, 0)),
            ],
        ),
        out_shape=[
            jax.ShapeDtypeStruct(shape, jnp.bfloat16),
            jax.ShapeDtypeStruct((groups, 128), jnp.float32),
        ],
        input_output_aliases={} if earlier is None else {2: 0},
        compiler_params=pltpu.CompilerParams(vmem_limit_bytes=VMEM),
        cost_estimate=pl.CostEstimate(flops=10**7, bytes_accessed=2 << 20, transcendentals=0),
    )(*operands)


def on_device(queries, new_keys, new_values, cache_keys, cache_values, cached_len, span_order):
    requests, tokens, heads, dim = queries.shape
    yz = lax.axis_index("yz")
    core = lax.axis_index("core")
    kv = lax.axis_index("kv")
    where = jnp.stack([yz * 2 + core, kv]).astype(jnp.int32)
    chips = lax.axis_size("yz")

    def other_core(x):
        return lax.ppermute(x, "core", [(0, 1), (1, 0)])

    k_own = cache_keys.reshape(requests, -1, dim)
    v_own = cache_values.reshape(requests, -1, dim)
    kn_own = new_keys.reshape(requests, -1, dim)
    vn_own = new_values.reshape(requests, -1, dim)
    q_own = queries.reshape(requests, tokens * heads, dim)
    k_par, v_par, kn_par, vn_par = (other_core(x) for x in (k_own, v_own, kn_own, vn_own))
    blocks = [q_own] + [
        lax.ppermute(q_own, "yz", [(c, c ^ s) for c in range(chips)]) for s in range(1, chips)
    ]
    vt, k_new = prepare(where, cached_len, v_own, v_par, vn_own, vn_par, kn_own, kn_par)

    received = []
    for r in range(requests):
        parts = attend(
            r, (0, 1, 2, 3), where, cached_len, span_order, blocks, k_own, k_par, k_new, vt
        )
        sent = parts.reshape((64,) + parts.shape[2:])
        got = lax.all_to_all(sent, ("yz", "kv"), 0, 0, tiled=True)
        received.append(got.reshape(parts.shape))
    attention = None
    norms = []
    for r in range(requests):
        attention, norm = combine(r, requests, where, received[r], attention)
        norms.append(norm[:, : tokens // 8 * heads].reshape(8, tokens // 8, heads))
    norm = jnp.stack(norms).transpose(0, 2, 1, 3).reshape(requests, tokens // 8, 8 * heads)
    return attention.reshape(requests, tokens // 8, 8 * heads, dim), norm


def solution(mesh):
    split = Mesh(mesh.devices.reshape(8, 2, 8), ("yz", "core", "kv"))
    placed = P(None, ("yz", "core"), "kv", None)
    return jax.shard_map(
        on_device,
        mesh=split,
        in_specs=(placed,) * 5 + (P(), P()),
        out_specs=(
            P(None, ("yz", "core", "kv"), None, None),
            P(None, ("yz", "core", "kv"), None),
        ),
        check_vma=False,
    )
```

```python
import functools

import jax
import jax.numpy as jnp
from jax import lax
from jax.experimental import pallas as pl
from jax.experimental.pallas import tpu as pltpu
from jax.sharding import Mesh
from jax.sharding import PartitionSpec as P

LOG2E = 1.4426950408889634
LN2 = 0.6931471805599453
MASKED = -1e30
SUM_LOW = 2.0**-60
SUM_HIGH = 2.0**100
VMEM = 56 << 20


def dot_nt(a, b):
    return lax.dot_general(a, b, (((1,), (1,)), ((), ())), preferred_element_type=jnp.float32)


def my_place():
    y, z, core = lax.axis_index("y"), lax.axis_index("z"), lax.axis_index("core")
    return (y * 4 + z) * 2 + core, core, y, z, lax.axis_index("kv")


def prepare_kernel(len_ref, vo_ref, vp_ref, vt_ref):
    r = pl.program_id(0)
    rows = vo_ref.shape[1]
    extra = vt_ref.shape[1] - 128
    me, core = my_place()[:2]
    for part, ref in enumerate((vo_ref, vp_ref)):
        owner = me if part == 0 else me + 1 - 2 * core
        valid = len_ref[r] - owner * rows
        row_id = lax.broadcasted_iota(jnp.int32, (rows, 128), 0)
        kept = jnp.where(row_id < valid, ref[0].astype(jnp.float32), 0.0).astype(jnp.bfloat16)
        vt_ref[0, :128, part * rows : (part + 1) * rows] = jnp.transpose(kept)
        col_id = lax.broadcasted_iota(jnp.int32, (extra, rows), 1)
        vt_ref[0, 128:, part * rows : (part + 1) * rows] = jnp.where(
            col_id < valid, 1.0, 0.0
        ).astype(jnp.bfloat16)


def prepare(cached_len, v_own, v_par):
    requests, rows, dim = v_own.shape
    whole = pl.BlockSpec((1, rows, dim), lambda r, *_: (r, 0, 0))
    return pl.pallas_call(
        prepare_kernel,
        grid_spec=pltpu.PrefetchScalarGridSpec(
            num_scalar_prefetch=1,
            grid=(requests,),
            in_specs=[whole, whole],
            out_specs=pl.BlockSpec((1, 144, 2 * rows), lambda r, *_: (r, 0, 0)),
        ),
        out_shape=jax.ShapeDtypeStruct((requests, 144, 2 * rows), jnp.bfloat16),
        compiler_params=pltpu.CompilerParams(vmem_limit_bytes=VMEM),
        cost_estimate=pl.CostEstimate(flops=10**6, bytes_accessed=4 << 20, transcendentals=0),
    )(cached_len, v_own, v_par)


def attend_kernel(tiles, n_q, n_aliased, len_ref, span_ref, *refs):
    inputs = refs[: n_q + 5]
    n_out = 1 + max(tile[0] for tile in tiles) - min(tile[0] for tile in tiles)
    first_out = n_q + 5 + n_aliased
    out_refs = refs[first_out : first_out + n_out]
    scratch = refs[first_out + n_out :]
    ko_ref, kp_ref, no_ref, np_ref, vt_ref, q_buf, acc_ref, top_ref, stage, sem, in_sem = scratch
    requests = sorted({tile[0] for tile in tiles})
    lowest = requests[0]
    rows = ko_ref.shape[1]

    loads = {}

    def load(name, source, target):
        loads[name] = pltpu.make_async_copy(source, target, in_sem.at[len(loads)])
        loads[name].start()

    def load_q(t):
        for half, (source, part) in enumerate(tiles[t][2]):
            array = inputs[source] if part is None else inputs[source].at[part]
            load(("q", t, half), array.at[tiles[t][0]], q_buf.at[t, half])

    def load_v(n):
        for r in requests:
            part = pl.ds(n * rows, rows)
            load(("v", n, r), inputs[n_q + 4].at[r, :, part], vt_ref.at[r - lowest, :, part])

    def load_k(name, index, ref):
        for r in requests:
            load((name, 0, r), inputs[n_q + index].at[r], ref.at[r - lowest])

    load_q(0)
    load_k("ko", 0, ko_ref)
    load_v(0)
    load_k("kp", 1, kp_ref)
    load_v(1)
    load_k("no", 2, no_ref)
    load_k("np", 3, np_ref)
    for t in range(1, len(tiles)):
        load_q(t)
    arrived = set()

    def need(*names):
        for name in names:
            if name not in arrived:
                arrived.add(name)
                loads[name].wait()

    me, core, my_y, my_z, _ = my_place()
    partner = me + 1 - 2 * core
    n_new = 2 * no_ref.shape[2]
    block = q_buf.shape[2]
    width = 2 * block
    scale = LOG2E * 128**-0.5

    def of_tile(t, field):
        if isinstance(t, int):
            return tiles[t][field]
        value = jnp.int32(tiles[0][field])
        for n in range(1, len(tiles)):
            value = jnp.where(t == n, jnp.int32(tiles[n][field]), value)
        return value

    def new_visible(t):
        request, hop = of_tile(t, 0), of_tile(t, 1)
        lane = lax.broadcasted_iota(jnp.int32, (1, width), 1)
        key = lax.broadcasted_iota(jnp.int32, (n_new, 1), 0)
        q_span = jnp.zeros((1, width), jnp.int32)
        k_span = jnp.zeros((n_new, 1), jnp.int32)
        first = jnp.int32(1 << 30)
        for n in range(4):
            source = 2 * ((my_y ^ (n // 2)) * 4 + (my_z ^ hop)) + core
            chosen = span_ref[request, 2 * source + n % 2]
            q_span = jnp.where(lane // (block // 2) == n, chosen, q_span)
            held = span_ref[request, 2 * (me if n < 2 else partner) + n % 2]
            k_span = jnp.where(key // 16 == n, held, k_span)
            first = jnp.minimum(first, held * 16)
        q_pos = q_span * 16 + lax.rem(lane // 16, 16)
        shown = (k_span * 16 + lax.rem(key, 16)) <= q_pos
        cached = len_ref[request] - jnp.minimum(me, partner) * rows > 0
        return shown, (q_pos >= first) | cached

    def values(request, p, start, size):
        return jnp.dot(
            vt_ref[request - lowest, :, pl.ds(start, size)],
            p.astype(jnp.bfloat16),
            preferred_element_type=jnp.float32,
        )

    def new_keys(at):
        return jnp.concatenate([no_ref[at, 0], np_ref[at, 0]], 0)

    def new_values(at, p):
        fresh = [no_ref[at, 1].astype(jnp.float32), np_ref[at, 1].astype(jnp.float32)]
        fresh = jnp.concatenate(fresh + [jnp.zeros((128 - n_new, 128), jnp.float32)], 0)
        turned = jnp.concatenate(
            [jnp.transpose(fresh), jnp.ones((vt_ref.shape[1] - 128, 128), jnp.float32)], 0
        ).astype(jnp.bfloat16)
        return jnp.dot(
            turned[:, :n_new], p.astype(jnp.bfloat16), preferred_element_type=jnp.float32
        )

    def send(t, request, hop):
        place = out_refs[request - lowest].at[my_z ^ hop]
        return pltpu.make_async_copy(stage.at[t], place, sem.at[t])

    def finish(t, acc, top):
        total = acc[128:129, :]
        some = total > 0.0
        safe = jnp.where(some, total, 1.0)
        inverse = jnp.where(some, 1.0 / safe, 0.0)
        outputs = jnp.transpose(acc[:128, :] * inverse).astype(jnp.bfloat16)
        log_total = jnp.where(some, (top + jnp.log2(safe)) * LN2, MASKED)
        high = log_total.astype(jnp.bfloat16).astype(jnp.float32)
        middle = (log_total - high).astype(jnp.bfloat16).astype(jnp.float32)
        low = log_total - high - middle
        logs = jnp.concatenate(
            [high, middle, low, jnp.zeros((5, width), jnp.float32)], 0
        ).astype(jnp.bfloat16)
        owners = stage.shape[2]
        share = block // owners
        for n in range(2):
            place = my_y ^ n
            stage[t, place, :, :share, :] = outputs[n * block : (n + 1) * block].reshape(
                owners, share, 128
            )
            for owner in range(owners):
                start = n * block + owner * share // 128 * 128
                stage[t, place, owner, share:, :] = logs[:, start : start + 128]

    worst = jnp.ones((1, width), jnp.int32)
    for t, (request, hop, source) in enumerate(tiles):
        at = request - lowest
        need(("q", t, 0), ("q", t, 1), ("ko", 0, request))
        q = q_buf[t].reshape(width, 128)
        p = jnp.exp2(dot_nt(ko_ref[at], q) * scale)
        need(("v", 0, request))
        acc = values(request, p, 0, rows)
        need(("kp", 0, request), ("v", 1, request))
        acc = acc + values(request, jnp.exp2(dot_nt(kp_ref[at], q) * scale), rows, rows)
        need(("no", 0, request), ("np", 0, request))
        shown, has_key = new_visible(t)
        s_new = jnp.where(shown, dot_nt(new_keys(at), q) * scale, MASKED)
        acc = acc + new_values(at, jnp.exp2(s_new))
        total = acc[128:129, :]
        fine = (total < SUM_HIGH) & ((total > SUM_LOW) | jnp.logical_not(has_key))
        worst = jnp.minimum(worst, jnp.where(fine, 1, 0))
        finish(t, acc, jnp.zeros((1, width), jnp.float32))
        send(t, request, hop).start()

    @pl.when(jnp.min(worst) == 0)
    def _():
        part = 256
        for t, (request, hop, _) in enumerate(tiles):
            send(t, request, hop).wait()

        def again(t, carry):
            request = of_tile(t, 0)
            q = q_buf[t].reshape(width, 128)
            shown, _ = new_visible(t)
            s_new = jnp.where(shown, dot_nt(new_keys(request - lowest), q) * scale, MASKED)

            def highest(ref, valid, top):
                def body(j, top):
                    s = dot_nt(ref[request - lowest, pl.ds(j * part, part), :], q) * scale
                    row = lax.broadcasted_iota(jnp.int32, (part, width), 0) + j * part
                    s = jnp.where(row < valid, s, MASKED)
                    return jnp.maximum(top, jnp.max(s, 0, keepdims=True))

                return lax.fori_loop(0, rows // part, body, top)

            top = jnp.max(s_new, 0, keepdims=True)
            top = highest(ko_ref, len_ref[request] - me * rows, top)
            top = highest(kp_ref, len_ref[request] - partner * rows, top)
            p_new = jnp.where(shown, jnp.exp2(jnp.minimum(s_new - top, 0.0)), 0.0)
            acc_ref[...] = new_values(request - lowest, p_new)

            def add(ref, first):
                def body(j, carry):
                    s = dot_nt(ref[request - lowest, pl.ds(j * part, part), :], q) * scale
                    start = pl.multiple_of(first + j * part, part)
                    acc_ref[...] += values(
                        request, jnp.exp2(jnp.minimum(s - top, 0.0)), start, part
                    )
                    return carry

                lax.fori_loop(0, rows // part, body, 0)

            add(ko_ref, 0)
            add(kp_ref, rows)
            top_ref[...] = jnp.broadcast_to(top, top_ref.shape)
            finish(t, acc_ref[...], top_ref[0:1, :])
            return carry

        lax.fori_loop(0, len(tiles), again, 0)
        for t, (request, hop, _) in enumerate(tiles):
            send(t, request, hop).start()

    for t, (request, hop, _) in enumerate(tiles):
        send(t, request, hop).wait()


def attend(tiles, cached_len, span_order, q_arrays, k_own, k_par, n_own, n_par, vt, partials):
    rows = k_own.shape[1]
    block = q_arrays[0].shape[-2]
    owners = 8
    share = block // owners
    width = 2 * block
    requests = sorted({tile[0] for tile in tiles})
    result = jax.ShapeDtypeStruct((4, 2, owners, share + 8, 128), jnp.bfloat16)
    keys = (k_own, k_par, n_own, n_par, vt)
    n_in = len(q_arrays) + len(keys)
    return pl.pallas_call(
        functools.partial(attend_kernel, tiles, len(q_arrays), len(partials)),
        in_specs=[pl.BlockSpec(memory_space=pltpu.SMEM)] * 2
        + [pl.BlockSpec(memory_space=pl.ANY)] * (n_in + len(partials)),
        out_specs=[pl.BlockSpec(memory_space=pl.ANY)] * len(requests),
        scratch_shapes=[pltpu.VMEM((len(requests),) + x.shape[1:], x.dtype) for x in keys]
        + [
            pltpu.VMEM((len(tiles), 2, block, 128), jnp.bfloat16),
            pltpu.VMEM((144, width), jnp.float32),
            pltpu.VMEM((8, width), jnp.float32),
            pltpu.VMEM((len(tiles), 2, owners, share + 8, 128), jnp.bfloat16),
            pltpu.SemaphoreType.DMA((len(tiles),)),
            pltpu.SemaphoreType.DMA((len(requests) * 6 + 2 * len(tiles),)),
        ],
        out_shape=[result] * len(requests),
        input_output_aliases={2 + n_in + n: n for n in range(len(partials))},
        compiler_params=pltpu.CompilerParams(vmem_limit_bytes=VMEM),
        cost_estimate=pl.CostEstimate(
            flops=len(tiles) * width * 2 * rows * 128 * 4,
            bytes_accessed=6 << 20,
            transcendentals=len(tiles) * width * 2 * rows,
        ),
    )(cached_len, span_order, *q_arrays, *keys, *partials)


def combine_kernel(request, in_ref, *refs):
    out_ref, norm_ref, held, sem = refs[-4:]
    sources, groups, rows, dim = held.shape
    share = rows - 8
    odd = lax.rem(lax.axis_index("kv"), 2) == 1
    copy = pltpu.make_async_copy(in_ref, held, sem)
    copy.start()
    lane = lax.broadcasted_iota(jnp.int32, (share, 128), 1)
    diagonal = lax.rem(lane, share) == lax.broadcasted_iota(jnp.int32, (share, 128), 0)
    shape = (sources, groups, 128)
    upper = lax.broadcasted_iota(jnp.int32, shape, 2) >= 64
    odd_source = lax.rem(lax.broadcasted_iota(jnp.int32, shape, 0), 2) == 1
    copy.wait()
    logs = held[:, :, share:, :].astype(jnp.float32)
    logs = logs[:, :, 0, :] + logs[:, :, 1, :] + logs[:, :, 2, :]
    turned = jnp.concatenate([logs[..., 64:], logs[..., :64]], 2)
    logs = jnp.where(upper == odd, logs, turned)
    highest = jnp.max(logs, 0)
    weight = jnp.exp(logs - highest[None])
    total = jnp.sum(weight, 0)
    norm = highest + jnp.log(total)
    shares = jnp.where(upper == odd_source, weight / total[None], 0.0)
    tokens = out_ref.shape[1]
    for group in range(groups):
        spread = jnp.concatenate(
            [
                jnp.where(
                    diagonal,
                    shares[n, group : group + 1] + shares[n + 1, group : group + 1],
                    0.0,
                )
                for n in range(0, sources, 2)
            ],
            1,
        )
        high = spread.astype(jnp.bfloat16)
        low = (spread - high.astype(jnp.float32)).astype(jnp.bfloat16)
        values = held[:, group, :share, :].reshape(sources * share, dim)
        summed = jnp.dot(high, values, preferred_element_type=jnp.float32) + jnp.dot(
            low, values, preferred_element_type=jnp.float32
        )
        out_ref[0, :, group] = summed.reshape(tokens, share // tokens, dim).astype(jnp.bfloat16)
    wide = share // tokens
    for token in range(tokens):
        norm_ref[0, token : token + 1, :] = jnp.concatenate(
            [norm[n : n + 1, token * wide : (token + 1) * wide] for n in range(groups)], 1
        )


def combine(request, requests, parts, earlier):
    sources, groups, rows, dim = parts.shape
    share = rows - 8
    tokens = share // 16
    shape = (requests, tokens, groups, 16, dim)
    return pl.pallas_call(
        functools.partial(combine_kernel, request),
        grid=(1,),
        in_specs=[pl.BlockSpec(memory_space=pl.ANY)] * (1 + len(earlier)),
        out_specs=[
            pl.BlockSpec((1,) + shape[1:], lambda *_: (request, 0, 0, 0, 0)),
            pl.BlockSpec((1, tokens, groups * 16), lambda *_: (request, 0, 0)),
        ],
        scratch_shapes=[
            pltpu.VMEM(parts.shape, parts.dtype),
            pltpu.SemaphoreType.DMA,
        ],
        out_shape=[
            jax.ShapeDtypeStruct(shape, jnp.bfloat16),
            jax.ShapeDtypeStruct((requests, tokens, groups * 16), jnp.float32),
        ],
        input_output_aliases={1 + n: n for n in range(len(earlier))},
        compiler_params=pltpu.CompilerParams(vmem_limit_bytes=63 << 20),
        cost_estimate=pl.CostEstimate(flops=10**7, bytes_accessed=2 << 20, transcendentals=0),
    )(parts, *earlier)


def on_device(queries, new_keys, new_values, cache_keys, cache_values, cached_len, span_order):
    requests, tokens, heads, dim = queries.shape

    def swapped(x, axis, flip=1):
        size = lax.axis_size(axis)
        return lax.ppermute(x, axis, [(n, n ^ flip) for n in range(size)])

    k_own = cache_keys.reshape(requests, -1, dim)
    v_own = cache_values.reshape(requests, -1, dim)
    n_own = jnp.stack(
        [new_keys.reshape(requests, -1, dim), new_values.reshape(requests, -1, dim)], 1
    )
    q_own = queries.reshape(requests, tokens * heads, dim)
    v_par = swapped(v_own, "core")
    q_other = swapped(q_own, "y")
    near = [swapped(q_own, "z", flip) for flip in (1, 3)]
    k_par = swapped(k_own, "core")
    n_par = swapped(n_own, "core")
    vt = prepare(cached_len, v_own, v_par)
    q_other, vt, near = lax.optimization_barrier((q_other, vt, near))
    next_to = [swapped(q_other, "z", flip) for flip in (1, 3)]
    far = swapped(jnp.stack([q_own, q_other]), "z", 2)

    common = (cached_len, span_order)
    keys = (k_own, k_par, n_own, n_par, vt)
    here = ((0, None), (1, None))
    partials = attend(
        tuple((r, 0, here) for r in range(requests)), *common, [q_own, q_other], *keys, []
    )
    hops = [near[0], next_to[0], near[1], next_to[1], far]
    received = []
    for r in range(requests):
        tiles = (
            (r, 1, ((0, None), (1, None))),
            (r, 3, ((2, None), (3, None))),
            (r, 2, ((4, 0), (4, 1))),
        )
        (parts,) = attend(tiles, *common, hops, *keys, [partials[r]])
        sent = parts.reshape((64,) + parts.shape[3:])
        got = lax.all_to_all(sent, ("z", "y", "kv"), 0, 0, tiled=True)
        received.append(got.reshape((8, 8) + parts.shape[3:]))
    results = []
    for r in range(requests):
        results = combine(r, requests, received[r], results)
    attention, norm = results
    return attention.reshape(requests, tokens // 8, 8 * heads, dim), norm


def solution(mesh):
    split = Mesh(mesh.devices.reshape(2, 4, 2, 8), ("y", "z", "core", "kv"))
    ctx = ("y", "z", "core")
    placed = P(None, ctx, "kv", None)
    return jax.shard_map(
        on_device,
        mesh=split,
        in_specs=(placed,) * 5 + (P(), P()),
        out_specs=(
            P(None, ctx + ("kv",), None, None),
            P(None, ctx + ("kv",), None),
        ),
        check_vma=False,
    )
```

```python
import functools

import jax
import jax.numpy as jnp
from jax import lax
from jax.experimental import pallas as pl
from jax.experimental.pallas import tpu as pltpu
from jax.sharding import Mesh
from jax.sharding import PartitionSpec as P

LOG2E = 1.4426950408889634
LN2 = 0.6931471805599453
MASKED = -1e30
SUM_LOW = 2.0**-60
SUM_HIGH = 2.0**100
VMEM = 56 << 20


def dot_nt(a, b):
    return lax.dot_general(a, b, (((1,), (1,)), ((), ())), preferred_element_type=jnp.float32)


def my_place():
    y, z, core = lax.axis_index("y"), lax.axis_index("z"), lax.axis_index("core")
    return (y * 4 + z) * 2 + core, core, y, z, lax.axis_index("kv")


def prepare_kernel(len_ref, vo_ref, vp_ref, vt_ref):
    r = pl.program_id(0)
    rows = vo_ref.shape[1]
    extra = vt_ref.shape[1] - 128
    me, core = my_place()[:2]
    for part, ref in enumerate((vo_ref, vp_ref)):
        owner = me if part == 0 else me + 1 - 2 * core
        valid = len_ref[r] - owner * rows
        row_id = lax.broadcasted_iota(jnp.int32, (rows, 128), 0)
        kept = jnp.where(row_id < valid, ref[0].astype(jnp.float32), 0.0).astype(jnp.bfloat16)
        vt_ref[0, :128, part * rows : (part + 1) * rows] = jnp.transpose(kept)
        col_id = lax.broadcasted_iota(jnp.int32, (extra, rows), 1)
        vt_ref[0, 128:, part * rows : (part + 1) * rows] = jnp.where(
            col_id < valid, 1.0, 0.0
        ).astype(jnp.bfloat16)


def prepare(cached_len, v_own, v_par):
    requests, rows, dim = v_own.shape
    whole = pl.BlockSpec((1, rows, dim), lambda r, *_: (r, 0, 0))
    return pl.pallas_call(
        prepare_kernel,
        grid_spec=pltpu.PrefetchScalarGridSpec(
            num_scalar_prefetch=1,
            grid=(requests,),
            in_specs=[whole, whole],
            out_specs=pl.BlockSpec((1, 144, 2 * rows), lambda r, *_: (r, 0, 0)),
        ),
        out_shape=jax.ShapeDtypeStruct((requests, 144, 2 * rows), jnp.bfloat16),
        compiler_params=pltpu.CompilerParams(vmem_limit_bytes=VMEM),
        cost_estimate=pl.CostEstimate(flops=10**6, bytes_accessed=4 << 20, transcendentals=0),
    )(cached_len, v_own, v_par)


def attend_kernel(tiles, n_q, n_aliased, len_ref, span_ref, *refs):
    inputs = refs[: n_q + 5]
    n_out = 1 + max(tile[0] for tile in tiles) - min(tile[0] for tile in tiles)
    first_out = n_q + 5 + n_aliased
    out_refs = refs[first_out : first_out + n_out]
    scratch = refs[first_out + n_out :]
    ko_ref, kp_ref, no_ref, np_ref, vt_ref, q_buf, acc_ref, top_ref, stage, sem, in_sem, q_sem = scratch
    requests = sorted({tile[0] for tile in tiles})
    lowest = requests[0]
    rows = ko_ref.shape[1]

    loads = {}

    def load(name, source, target):
        loads[name] = pltpu.make_async_copy(source, target, in_sem.at[len(loads)])
        loads[name].start()

    def fetch(request, t, half, source=0, part=None):
        array = inputs[source] if part is None else inputs[source].at[part]
        return pltpu.make_async_copy(array.at[request], q_buf.at[t, half], q_sem.at[2 * t + half])

    def load_q(t):
        for half, (source, part) in enumerate(tiles[t][2]):
            fetch(tiles[t][0], t, half, source, part).start()

    def load_v(n):
        for r in requests:
            part = pl.ds(n * rows, rows)
            load(("v", n, r), inputs[n_q + 4].at[r, :, part], vt_ref.at[r - lowest, :, part])

    def load_k(name, index, ref):
        for r in requests:
            load((name, 0, r), inputs[n_q + index].at[r], ref.at[r - lowest])

    load_q(0)
    load_k("ko", 0, ko_ref)
    load_v(0)
    load_k("kp", 1, kp_ref)
    load_v(1)
    load_k("no", 2, no_ref)
    load_k("np", 3, np_ref)
    for t in range(1, len(tiles)):
        load_q(t)
    me, core, my_y, my_z, _ = my_place()
    partner = me + 1 - 2 * core
    n_new = 2 * no_ref.shape[2]
    block = q_buf.shape[2]
    width = 2 * block
    scale = LOG2E * 128**-0.5

    def of_tile(t, field):
        if isinstance(t, int):
            return tiles[t][field]
        value = jnp.int32(tiles[0][field])
        for n in range(1, len(tiles)):
            value = jnp.where(t == n, jnp.int32(tiles[n][field]), value)
        return value

    def new_visible(t):
        request, hop = of_tile(t, 0), of_tile(t, 1)
        lane = lax.broadcasted_iota(jnp.int32, (1, width), 1)
        key = lax.broadcasted_iota(jnp.int32, (n_new, 1), 0)
        q_span = jnp.zeros((1, width), jnp.int32)
        k_span = jnp.zeros((n_new, 1), jnp.int32)
        first = jnp.int32(1 << 30)
        for n in range(4):
            source = 2 * ((my_y ^ (n // 2)) * 4 + (my_z ^ hop)) + core
            chosen = span_ref[request, 2 * source + n % 2]
            q_span = jnp.where(lane // (block // 2) == n, chosen, q_span)
            held = span_ref[request, 2 * (me if n < 2 else partner) + n % 2]
            k_span = jnp.where(key // 16 == n, held, k_span)
            first = jnp.minimum(first, held * 16)
        q_pos = q_span * 16 + lax.rem(lane // 16, 16)
        shown = (k_span * 16 + lax.rem(key, 16)) <= q_pos
        cached = len_ref[request] - jnp.minimum(me, partner) * rows > 0
        return shown, (q_pos >= first) | cached

    def values(request, p, start, size):
        return jnp.dot(
            vt_ref[request - lowest, :, pl.ds(start, size)],
            p.astype(jnp.bfloat16),
            preferred_element_type=jnp.float32,
        )

    def new_keys(at):
        return jnp.concatenate([no_ref[at, 0], np_ref[at, 0]], 0)

    def new_values(at, p):
        fresh = [no_ref[at, 1].astype(jnp.float32), np_ref[at, 1].astype(jnp.float32)]
        fresh = jnp.concatenate(fresh + [jnp.zeros((128 - n_new, 128), jnp.float32)], 0)
        turned = jnp.concatenate(
            [jnp.transpose(fresh), jnp.ones((vt_ref.shape[1] - 128, 128), jnp.float32)], 0
        ).astype(jnp.bfloat16)
        return jnp.dot(
            turned[:, :n_new], p.astype(jnp.bfloat16), preferred_element_type=jnp.float32
        )

    def send(t, request, hop):
        place = out_refs[request - lowest].at[my_z ^ hop]
        return pltpu.make_async_copy(stage.at[t], place, sem.at[t])

    def finish(t, acc, top):
        total = acc[128:129, :]
        some = total > 0.0
        safe = jnp.where(some, total, 1.0)
        inverse = jnp.where(some, 1.0 / safe, 0.0)
        outputs = jnp.transpose(acc[:128, :] * inverse).astype(jnp.bfloat16)
        log_total = jnp.where(some, (top + jnp.log2(safe)) * LN2, MASKED)
        high = log_total.astype(jnp.bfloat16).astype(jnp.float32)
        middle = (log_total - high).astype(jnp.bfloat16).astype(jnp.float32)
        low = log_total - high - middle
        logs = jnp.concatenate(
            [high, middle, low, jnp.zeros((5, width), jnp.float32)], 0
        ).astype(jnp.bfloat16)
        owners = stage.shape[2]
        share = block // owners
        for n in range(2):
            place = my_y ^ n
            stage[t, place, :, :share, :] = outputs[n * block : (n + 1) * block].reshape(
                owners, share, 128
            )
            for owner in range(owners):
                start = n * block + owner * share // 128 * 128
                stage[t, place, owner, share:, :] = logs[:, start : start + 128]

    for r in requests:
        for name, n in (("ko", 0), ("v", 0), ("kp", 0), ("v", 1), ("no", 0), ("np", 0)):
            loads[name, n, r].wait()

    def whole_tile(t, worst):
        request = of_tile(t, 0)
        at = request - lowest
        for half in range(2):
            fetch(0, t, half).wait()
        q = q_buf[t].reshape(width, 128)
        acc = values(request, jnp.exp2(dot_nt(ko_ref[at], q) * scale), 0, rows)
        acc = acc + values(request, jnp.exp2(dot_nt(kp_ref[at], q) * scale), rows, rows)
        shown, has_key = new_visible(t)
        s_new = jnp.where(shown, dot_nt(new_keys(at), q) * scale, MASKED)
        acc = acc + new_values(at, jnp.exp2(s_new))
        total = acc[128:129, :]
        fine = (total < SUM_HIGH) & ((total > SUM_LOW) | jnp.logical_not(has_key))
        finish(t, acc, jnp.zeros((1, width), jnp.float32))
        return jnp.minimum(worst, jnp.where(fine, 1, 0))

    worst = lax.fori_loop(0, len(tiles), whole_tile, jnp.ones((1, width), jnp.int32))

    @pl.when(jnp.min(worst) == 0)
    def _():
        part = 256

        def again(t, carry):
            request = of_tile(t, 0)
            q = q_buf[t].reshape(width, 128)
            shown, _ = new_visible(t)
            s_new = jnp.where(shown, dot_nt(new_keys(request - lowest), q) * scale, MASKED)

            def highest(ref, valid, top):
                def body(j, top):
                    s = dot_nt(ref[request - lowest, pl.ds(j * part, part), :], q) * scale
                    row = lax.broadcasted_iota(jnp.int32, (part, width), 0) + j * part
                    s = jnp.where(row < valid, s, MASKED)
                    return jnp.maximum(top, jnp.max(s, 0, keepdims=True))

                return lax.fori_loop(0, rows // part, body, top)

            top = jnp.max(s_new, 0, keepdims=True)
            top = highest(ko_ref, len_ref[request] - me * rows, top)
            top = highest(kp_ref, len_ref[request] - partner * rows, top)
            p_new = jnp.where(shown, jnp.exp2(jnp.minimum(s_new - top, 0.0)), 0.0)
            acc_ref[...] = new_values(request - lowest, p_new)

            def add(ref, first):
                def body(j, carry):
                    s = dot_nt(ref[request - lowest, pl.ds(j * part, part), :], q) * scale
                    start = pl.multiple_of(first + j * part, part)
                    acc_ref[...] += values(
                        request, jnp.exp2(jnp.minimum(s - top, 0.0)), start, part
                    )
                    return carry

                lax.fori_loop(0, rows // part, body, 0)

            add(ko_ref, 0)
            add(kp_ref, rows)
            top_ref[...] = jnp.broadcast_to(top, top_ref.shape)
            finish(t, acc_ref[...], top_ref[0:1, :])
            return carry

        lax.fori_loop(0, len(tiles), again, 0)

    for t, (request, hop, _) in enumerate(tiles):
        send(t, request, hop).start()
    for t, (request, hop, _) in enumerate(tiles):
        send(t, request, hop).wait()


def attend(tiles, cached_len, span_order, q_arrays, k_own, k_par, n_own, n_par, vt, partials):
    rows = k_own.shape[1]
    block = q_arrays[0].shape[-2]
    owners = 8
    share = block // owners
    width = 2 * block
    requests = sorted({tile[0] for tile in tiles})
    result = jax.ShapeDtypeStruct((4, 2, owners, share + 8, 128), jnp.bfloat16)
    keys = (k_own, k_par, n_own, n_par, vt)
    n_in = len(q_arrays) + len(keys)
    return pl.pallas_call(
        functools.partial(attend_kernel, tiles, len(q_arrays), len(partials)),
        in_specs=[pl.BlockSpec(memory_space=pltpu.SMEM)] * 2
        + [pl.BlockSpec(memory_space=pl.ANY)] * (n_in + len(partials)),
        out_specs=[pl.BlockSpec(memory_space=pl.ANY)] * len(requests),
        scratch_shapes=[pltpu.VMEM((len(requests),) + x.shape[1:], x.dtype) for x in keys]
        + [
            pltpu.VMEM((len(tiles), 2, block, 128), jnp.bfloat16),
            pltpu.VMEM((144, width), jnp.float32),
            pltpu.VMEM((8, width), jnp.float32),
            pltpu.VMEM((len(tiles), 2, owners, share + 8, 128), jnp.bfloat16),
            pltpu.SemaphoreType.DMA((len(tiles),)),
            pltpu.SemaphoreType.DMA((len(requests) * 6,)),
            pltpu.SemaphoreType.DMA((2 * len(tiles),)),
        ],
        out_shape=[result] * len(requests),
        input_output_aliases={2 + n_in + n: n for n in range(len(partials))},
        compiler_params=pltpu.CompilerParams(vmem_limit_bytes=VMEM),
        cost_estimate=pl.CostEstimate(
            flops=len(tiles) * width * 2 * rows * 128 * 4,
            bytes_accessed=6 << 20,
            transcendentals=len(tiles) * width * 2 * rows,
        ),
    )(cached_len, span_order, *q_arrays, *keys, *partials)


def combine_kernel(request, in_ref, *refs):
    out_ref, norm_ref, held, sem = refs[-4:]
    sources, groups, rows, dim = held.shape
    share = rows - 8
    odd = lax.rem(lax.axis_index("kv"), 2) == 1
    copy = pltpu.make_async_copy(in_ref, held, sem)
    copy.start()
    lane = lax.broadcasted_iota(jnp.int32, (share, 128), 1)
    diagonal = lax.rem(lane, share) == lax.broadcasted_iota(jnp.int32, (share, 128), 0)
    shape = (sources, groups, 128)
    upper = lax.broadcasted_iota(jnp.int32, shape, 2) >= 64
    odd_source = lax.rem(lax.broadcasted_iota(jnp.int32, shape, 0), 2) == 1
    copy.wait()
    logs = held[:, :, share:, :].astype(jnp.float32)
    logs = logs[:, :, 0, :] + logs[:, :, 1, :] + logs[:, :, 2, :]
    turned = jnp.concatenate([logs[..., 64:], logs[..., :64]], 2)
    logs = jnp.where(upper == odd, logs, turned)
    highest = jnp.max(logs, 0)
    weight = jnp.exp(logs - highest[None])
    total = jnp.sum(weight, 0)
    norm = highest + jnp.log(total)
    shares = jnp.where(upper == odd_source, weight / total[None], 0.0)
    tokens = out_ref.shape[1]
    for group in range(groups):
        spread = jnp.concatenate(
            [
                jnp.where(
                    diagonal,
                    shares[n, group : group + 1] + shares[n + 1, group : group + 1],
                    0.0,
                )
                for n in range(0, sources, 2)
            ],
            1,
        )
        high = spread.astype(jnp.bfloat16)
        low = (spread - high.astype(jnp.float32)).astype(jnp.bfloat16)
        values = held[:, group, :share, :].reshape(sources * share, dim)
        summed = jnp.dot(high, values, preferred_element_type=jnp.float32) + jnp.dot(
            low, values, preferred_element_type=jnp.float32
        )
        out_ref[0, :, group] = summed.reshape(tokens, share // tokens, dim).astype(jnp.bfloat16)
    wide = share // tokens
    for token in range(tokens):
        norm_ref[0, token : token + 1, :] = jnp.concatenate(
            [norm[n : n + 1, token * wide : (token + 1) * wide] for n in range(groups)], 1
        )


def combine(request, requests, parts, earlier):
    sources, groups, rows, dim = parts.shape
    share = rows - 8
    tokens = share // 16
    shape = (requests, tokens, groups, 16, dim)
    return pl.pallas_call(
        functools.partial(combine_kernel, request),
        grid=(1,),
        in_specs=[pl.BlockSpec(memory_space=pl.ANY)] * (1 + len(earlier)),
        out_specs=[
            pl.BlockSpec((1,) + shape[1:], lambda *_: (request, 0, 0, 0, 0)),
            pl.BlockSpec((1, tokens, groups * 16), lambda *_: (request, 0, 0)),
        ],
        scratch_shapes=[
            pltpu.VMEM(parts.shape, parts.dtype),
            pltpu.SemaphoreType.DMA,
        ],
        out_shape=[
            jax.ShapeDtypeStruct(shape, jnp.bfloat16),
            jax.ShapeDtypeStruct((requests, tokens, groups * 16), jnp.float32),
        ],
        input_output_aliases={1 + n: n for n in range(len(earlier))},
        compiler_params=pltpu.CompilerParams(vmem_limit_bytes=63 << 20),
        cost_estimate=pl.CostEstimate(flops=10**7, bytes_accessed=2 << 20, transcendentals=0),
    )(parts, *earlier)


def on_device(queries, new_keys, new_values, cache_keys, cache_values, cached_len, span_order):
    requests, tokens, heads, dim = queries.shape

    def swapped(x, axis, flip=1):
        size = lax.axis_size(axis)
        return lax.ppermute(x, axis, [(n, n ^ flip) for n in range(size)])

    k_own = cache_keys.reshape(requests, -1, dim)
    v_own = cache_values.reshape(requests, -1, dim)
    n_own = jnp.stack(
        [new_keys.reshape(requests, -1, dim), new_values.reshape(requests, -1, dim)], 1
    )
    q_own = queries.reshape(requests, tokens * heads, dim)
    v_par = swapped(v_own, "core")
    q_other = swapped(q_own, "y")
    near = [swapped(q_own, "z", flip) for flip in (1, 3)]
    k_par = swapped(k_own, "core")
    n_par = swapped(n_own, "core")
    vt = prepare(cached_len, v_own, v_par)
    q_other, vt, near = lax.optimization_barrier((q_other, vt, near))
    next_to = [swapped(q_other, "z", flip) for flip in (1, 3)]
    far = swapped(jnp.stack([q_own, q_other]), "z", 2)

    common = (cached_len, span_order)
    keys = (k_own, k_par, n_own, n_par, vt)
    here = ((0, None), (1, None))
    partials = attend(
        tuple((r, 0, here) for r in range(requests)), *common, [q_own, q_other], *keys, []
    )
    hops = [near[0], next_to[0], near[1], next_to[1], far]
    received = []
    for r in range(requests):
        tiles = (
            (r, 1, ((0, None), (1, None))),
            (r, 3, ((2, None), (3, None))),
            (r, 2, ((4, 0), (4, 1))),
        )
        (parts,) = attend(tiles, *common, hops, *keys, [partials[r]])
        sent = parts.reshape((64,) + parts.shape[3:])
        got = lax.all_to_all(sent, ("z", "y", "kv"), 0, 0, tiled=True)
        received.append(got.reshape((8, 8) + parts.shape[3:]))
    results = []
    for r in range(requests):
        results = combine(r, requests, received[r], results)
    attention, norm = results
    return attention.reshape(requests, tokens // 8, 8 * heads, dim), norm


def solution(mesh):
    split = Mesh(mesh.devices.reshape(2, 4, 2, 8), ("y", "z", "core", "kv"))
    ctx = ("y", "z", "core")
    placed = P(None, ctx, "kv", None)
    return jax.shard_map(
        on_device,
        mesh=split,
        in_specs=(placed,) * 5 + (P(), P()),
        out_specs=(
            P(None, ctx + ("kv",), None, None),
            P(None, ctx + ("kv",), None),
        ),
        check_vma=False,
    )
```

```python
import functools

import jax
import jax.numpy as jnp
from jax import lax
from jax.experimental import pallas as pl
from jax.experimental.pallas import tpu as pltpu
from jax.sharding import Mesh
from jax.sharding import PartitionSpec as P

LOG2E = 1.4426950408889634
LN2 = 0.6931471805599453
MASKED = -1e30
SUM_LOW = 2.0**-60
SUM_HIGH = 2.0**100
VMEM = 56 << 20


def dot_nt(a, b):
    return lax.dot_general(a, b, (((1,), (1,)), ((), ())), preferred_element_type=jnp.float32)


def my_place():
    y, z, core = lax.axis_index("y"), lax.axis_index("z"), lax.axis_index("core")
    return (y * 4 + z) * 2 + core, core, y, z, lax.axis_index("kv")


def prepare_kernel(len_ref, vo_ref, vp_ref, vt_ref):
    r = pl.program_id(0)
    rows = vo_ref.shape[1]
    extra = vt_ref.shape[1] - 128
    me, core = my_place()[:2]
    for part, ref in enumerate((vo_ref, vp_ref)):
        owner = me if part == 0 else me + 1 - 2 * core
        valid = len_ref[r] - owner * rows
        row_id = lax.broadcasted_iota(jnp.int32, (rows, 128), 0)
        kept = jnp.where(row_id < valid, ref[0].astype(jnp.float32), 0.0).astype(jnp.bfloat16)
        vt_ref[0, :128, part * rows : (part + 1) * rows] = jnp.transpose(kept)
        col_id = lax.broadcasted_iota(jnp.int32, (extra, rows), 1)
        vt_ref[0, 128:, part * rows : (part + 1) * rows] = jnp.where(
            col_id < valid, 1.0, 0.0
        ).astype(jnp.bfloat16)


def prepare(cached_len, v_own, v_par):
    requests, rows, dim = v_own.shape
    whole = pl.BlockSpec((1, rows, dim), lambda r, *_: (r, 0, 0))
    return pl.pallas_call(
        prepare_kernel,
        grid_spec=pltpu.PrefetchScalarGridSpec(
            num_scalar_prefetch=1,
            grid=(requests,),
            in_specs=[whole, whole],
            out_specs=pl.BlockSpec((1, 144, 2 * rows), lambda r, *_: (r, 0, 0)),
        ),
        out_shape=jax.ShapeDtypeStruct((requests, 144, 2 * rows), jnp.bfloat16),
        compiler_params=pltpu.CompilerParams(vmem_limit_bytes=VMEM),
        cost_estimate=pl.CostEstimate(flops=10**6, bytes_accessed=4 << 20, transcendentals=0),
    )(cached_len, v_own, v_par)


def attend_kernel(tiles, n_q, n_aliased, len_ref, span_ref, *refs):
    inputs = refs[: n_q + 5]
    n_out = 1 + max(tile[0] for tile in tiles) - min(tile[0] for tile in tiles)
    first_out = n_q + 5 + n_aliased
    out_refs = refs[first_out : first_out + n_out]
    scratch = refs[first_out + n_out :]
    ko_ref, kp_ref, no_ref, np_ref, vt_ref = scratch[:5]
    q_buf, acc_ref, top_ref, stage, sem, in_sem, q_sem = scratch[5:]
    requests = sorted({tile[0] for tile in tiles})
    lowest = requests[0]
    rows = ko_ref.shape[1]

    loads = {}

    def load(name, source, target):
        loads[name] = pltpu.make_async_copy(source, target, in_sem.at[len(loads)])
        loads[name].start()

    def fetch(request, t, half, source=0, part=None):
        array = inputs[source] if part is None else inputs[source].at[part]
        return pltpu.make_async_copy(array.at[request], q_buf.at[t, half], q_sem.at[2 * t + half])

    def load_q(t):
        for half in range(2):
            source, part = tiles[t][1 + half][2:]
            fetch(tiles[t][0], t, half, source, part).start()

    load_q(0)
    for r in requests:
        at = r - lowest
        load(("ko", 0, r), inputs[n_q].at[r], ko_ref.at[at])
        for n in range(2):
            part = pl.ds(n * rows, rows)
            load(("v", n, r), inputs[n_q + 4].at[r, :, part], vt_ref.at[at, :, part])
        load(("kp", 0, r), inputs[n_q + 1].at[r], kp_ref.at[at])
        load(("no", 0, r), inputs[n_q + 2].at[r], no_ref.at[at])
        load(("np", 0, r), inputs[n_q + 3].at[r], np_ref.at[at])
    for t in range(1, len(tiles)):
        load_q(t)
    me, core, my_y, my_z, _ = my_place()
    partner = me + 1 - 2 * core
    n_new = 2 * no_ref.shape[2]
    block = q_buf.shape[2]
    width = 2 * block
    scale = LOG2E * 128**-0.5

    def of_tile(t, choose):
        value = jnp.int32(choose(tiles[0]))
        for n in range(1, len(tiles)):
            value = jnp.where(t == n, jnp.int32(choose(tiles[n])), value)
        return value

    def request_of(t):
        return of_tile(t, lambda tile: tile[0])

    def new_visible(t):
        request = request_of(t)
        lane = lax.broadcasted_iota(jnp.int32, (1, width), 1)
        key = lax.broadcasted_iota(jnp.int32, (n_new, 1), 0)
        q_span = jnp.zeros((1, width), jnp.int32)
        k_span = jnp.zeros((n_new, 1), jnp.int32)
        first = jnp.int32(1 << 30)
        for n in range(4):
            hop_z = of_tile(t, lambda tile: tile[1 + n // 2][0])
            hop_y = of_tile(t, lambda tile: tile[1 + n // 2][1])
            source = 2 * ((my_y ^ hop_y) * 4 + (my_z ^ hop_z)) + core
            chosen = span_ref[request, 2 * source + n % 2]
            q_span = jnp.where(lane // (block // 2) == n, chosen, q_span)
            held = span_ref[request, 2 * (me if n < 2 else partner) + n % 2]
            k_span = jnp.where(key // 16 == n, held, k_span)
            first = jnp.minimum(first, held * 16)
        q_pos = q_span * 16 + lax.rem(lane // 16, 16)
        shown = (k_span * 16 + lax.rem(key, 16)) <= q_pos
        cached = len_ref[request] - jnp.minimum(me, partner) * rows > 0
        return shown, (q_pos >= first) | cached

    def values(request, p, start, size):
        return jnp.dot(
            vt_ref[request - lowest, :, pl.ds(start, size)],
            p.astype(jnp.bfloat16),
            preferred_element_type=jnp.float32,
        )

    def new_keys(at):
        return jnp.concatenate([no_ref[at, 0], np_ref[at, 0]], 0)

    def new_values(at, p):
        fresh = [no_ref[at, 1].astype(jnp.float32), np_ref[at, 1].astype(jnp.float32)]
        fresh = jnp.concatenate(fresh + [jnp.zeros((128 - n_new, 128), jnp.float32)], 0)
        turned = jnp.concatenate(
            [jnp.transpose(fresh), jnp.ones((vt_ref.shape[1] - 128, 128), jnp.float32)], 0
        ).astype(jnp.bfloat16)
        return jnp.dot(
            turned[:, :n_new], p.astype(jnp.bfloat16), preferred_element_type=jnp.float32
        )

    def sends():
        for t, (request, *halves) in enumerate(tiles):
            for half, (hop_z, hop_y, _, _) in enumerate(halves):
                place = out_refs[request - lowest].at[my_z ^ hop_z, my_y ^ hop_y]
                yield pltpu.make_async_copy(stage.at[t, half], place, sem.at[2 * t + half])

    def finish(t, acc, top):
        total = acc[128:129, :]
        some = total > 0.0
        safe = jnp.where(some, total, 1.0)
        inverse = jnp.where(some, 1.0 / safe, 0.0)
        outputs = jnp.transpose(acc[:128, :] * inverse).astype(jnp.bfloat16)
        log_total = jnp.where(some, (top + jnp.log2(safe)) * LN2, MASKED)
        high = log_total.astype(jnp.bfloat16).astype(jnp.float32)
        middle = (log_total - high).astype(jnp.bfloat16).astype(jnp.float32)
        low = log_total - high - middle
        logs = jnp.concatenate(
            [high, middle, low, jnp.zeros((5, width), jnp.float32)], 0
        ).astype(jnp.bfloat16)
        owners = stage.shape[2]
        share = block // owners
        for n in range(2):
            stage[t, n, :, :share, :] = outputs[n * block : (n + 1) * block].reshape(
                owners, share, 128
            )
            for owner in range(owners):
                start = n * block + owner * share // 128 * 128
                stage[t, n, owner, share:, :] = logs[:, start : start + 128]

    def whole_tile(t, worst):
        request = request_of(t)
        at = request - lowest
        for r in requests:

            @pl.when(t == [tile[0] for tile in tiles].index(r))
            def _(r=r):
                for name, n in (("ko", 0), ("v", 0), ("kp", 0), ("v", 1), ("no", 0), ("np", 0)):
                    loads[name, n, r].wait()

        for half in range(2):
            fetch(0, t, half).wait()
        q = q_buf[t].reshape(width, 128)
        acc = values(request, jnp.exp2(dot_nt(ko_ref[at], q) * scale), 0, rows)
        acc = acc + values(request, jnp.exp2(dot_nt(kp_ref[at], q) * scale), rows, rows)
        shown, has_key = new_visible(t)
        s_new = jnp.where(shown, dot_nt(new_keys(at), q) * scale, MASKED)
        acc = acc + new_values(at, jnp.exp2(s_new))
        total = acc[128:129, :]
        fine = (total < SUM_HIGH) & ((total > SUM_LOW) | jnp.logical_not(has_key))
        finish(t, acc, jnp.zeros((1, width), jnp.float32))
        return jnp.minimum(worst, jnp.where(fine, 1, 0))

    worst = lax.fori_loop(0, len(tiles), whole_tile, jnp.ones((1, width), jnp.int32))

    @pl.when(jnp.min(worst) == 0)
    def _():
        part = 256

        def again(t, carry):
            request = request_of(t)
            q = q_buf[t].reshape(width, 128)
            shown, _ = new_visible(t)
            s_new = jnp.where(shown, dot_nt(new_keys(request - lowest), q) * scale, MASKED)

            def highest(ref, valid, top):
                def body(j, top):
                    s = dot_nt(ref[request - lowest, pl.ds(j * part, part), :], q) * scale
                    row = lax.broadcasted_iota(jnp.int32, (part, width), 0) + j * part
                    s = jnp.where(row < valid, s, MASKED)
                    return jnp.maximum(top, jnp.max(s, 0, keepdims=True))

                return lax.fori_loop(0, rows // part, body, top)

            top = jnp.max(s_new, 0, keepdims=True)
            top = highest(ko_ref, len_ref[request] - me * rows, top)
            top = highest(kp_ref, len_ref[request] - partner * rows, top)
            p_new = jnp.where(shown, jnp.exp2(jnp.minimum(s_new - top, 0.0)), 0.0)
            acc_ref[...] = new_values(request - lowest, p_new)

            def add(ref, first):
                def body(j, carry):
                    s = dot_nt(ref[request - lowest, pl.ds(j * part, part), :], q) * scale
                    start = pl.multiple_of(first + j * part, part)
                    acc_ref[...] += values(
                        request, jnp.exp2(jnp.minimum(s - top, 0.0)), start, part
                    )
                    return carry

                lax.fori_loop(0, rows // part, body, 0)

            add(ko_ref, 0)
            add(kp_ref, rows)
            top_ref[...] = jnp.broadcast_to(top, top_ref.shape)
            finish(t, acc_ref[...], top_ref[0:1, :])
            return carry

        lax.fori_loop(0, len(tiles), again, 0)

    for copy in sends():
        copy.start()
    for copy in sends():
        copy.wait()


def attend(tiles, cached_len, span_order, q_arrays, k_own, k_par, n_own, n_par, vt, partials):
    rows = k_own.shape[1]
    block = q_arrays[0].shape[-2]
    owners = 8
    share = block // owners
    width = 2 * block
    requests = sorted({tile[0] for tile in tiles})
    result = jax.ShapeDtypeStruct((4, 2, owners, share + 8, 128), jnp.bfloat16)
    keys = (k_own, k_par, n_own, n_par, vt)
    n_in = len(q_arrays) + len(keys)
    return pl.pallas_call(
        functools.partial(attend_kernel, tiles, len(q_arrays), len(partials)),
        in_specs=[pl.BlockSpec(memory_space=pltpu.SMEM)] * 2
        + [pl.BlockSpec(memory_space=pl.ANY)] * (n_in + len(partials)),
        out_specs=[pl.BlockSpec(memory_space=pl.ANY)] * len(requests),
        scratch_shapes=[pltpu.VMEM((len(requests),) + x.shape[1:], x.dtype) for x in keys]
        + [
            pltpu.VMEM((len(tiles), 2, block, 128), jnp.bfloat16),
            pltpu.VMEM((144, width), jnp.float32),
            pltpu.VMEM((8, width), jnp.float32),
            pltpu.VMEM((len(tiles), 2, owners, share + 8, 128), jnp.bfloat16),
            pltpu.SemaphoreType.DMA((2 * len(tiles),)),
            pltpu.SemaphoreType.DMA((len(requests) * 6,)),
            pltpu.SemaphoreType.DMA((2 * len(tiles),)),
        ],
        out_shape=[result] * len(requests),
        input_output_aliases={2 + n_in + n: n for n in range(len(partials))},
        compiler_params=pltpu.CompilerParams(vmem_limit_bytes=VMEM),
        cost_estimate=pl.CostEstimate(
            flops=len(tiles) * width * 2 * rows * 128 * 4,
            bytes_accessed=6 << 20,
            transcendentals=len(tiles) * width * 2 * rows,
        ),
    )(cached_len, span_order, *q_arrays, *keys, *partials)


def combine_kernel(request, in_ref, *refs):
    out_ref, norm_ref, held, sem = refs[-4:]
    sources, groups, rows, dim = held.shape
    share = rows - 8
    odd = lax.rem(lax.axis_index("kv"), 2) == 1
    copy = pltpu.make_async_copy(in_ref, held, sem)
    copy.start()
    lane = lax.broadcasted_iota(jnp.int32, (share, 128), 1)
    diagonal = lax.rem(lane, share) == lax.broadcasted_iota(jnp.int32, (share, 128), 0)
    shape = (sources, groups, 128)
    upper = lax.broadcasted_iota(jnp.int32, shape, 2) >= 64
    odd_source = lax.rem(lax.broadcasted_iota(jnp.int32, shape, 0), 2) == 1
    copy.wait()
    logs = held[:, :, share:, :].astype(jnp.float32)
    logs = logs[:, :, 0, :] + logs[:, :, 1, :] + logs[:, :, 2, :]
    turned = jnp.concatenate([logs[..., 64:], logs[..., :64]], 2)
    logs = jnp.where(upper == odd, logs, turned)
    highest = jnp.max(logs, 0)
    weight = jnp.exp(logs - highest[None])
    total = jnp.sum(weight, 0)
    norm = highest + jnp.log(total)
    shares = jnp.where(upper == odd_source, weight / total[None], 0.0)
    tokens = out_ref.shape[1]
    for group in range(groups):
        spread = jnp.concatenate(
            [
                jnp.where(
                    diagonal,
                    shares[n, group : group + 1] + shares[n + 1, group : group + 1],
                    0.0,
                )
                for n in range(0, sources, 2)
            ],
            1,
        )
        high = spread.astype(jnp.bfloat16)
        low = (spread - high.astype(jnp.float32)).astype(jnp.bfloat16)
        values = held[:, group, :share, :].reshape(sources * share, dim)
        summed = jnp.dot(high, values, preferred_element_type=jnp.float32) + jnp.dot(
            low, values, preferred_element_type=jnp.float32
        )
        out_ref[0, :, group] = summed.reshape(tokens, share // tokens, dim).astype(jnp.bfloat16)
    wide = share // tokens
    for token in range(tokens):
        norm_ref[0, token : token + 1, :] = jnp.concatenate(
            [norm[n : n + 1, token * wide : (token + 1) * wide] for n in range(groups)], 1
        )


def combine(request, requests, parts, earlier):
    sources, groups, rows, dim = parts.shape
    share = rows - 8
    tokens = share // 16
    shape = (requests, tokens, groups, 16, dim)
    return pl.pallas_call(
        functools.partial(combine_kernel, request),
        grid=(1,),
        in_specs=[pl.BlockSpec(memory_space=pl.ANY)] * (1 + len(earlier)),
        out_specs=[
            pl.BlockSpec((1,) + shape[1:], lambda *_: (request, 0, 0, 0, 0)),
            pl.BlockSpec((1, tokens, groups * 16), lambda *_: (request, 0, 0)),
        ],
        scratch_shapes=[
            pltpu.VMEM(parts.shape, parts.dtype),
            pltpu.SemaphoreType.DMA,
        ],
        out_shape=[
            jax.ShapeDtypeStruct(shape, jnp.bfloat16),
            jax.ShapeDtypeStruct((requests, tokens, groups * 16), jnp.float32),
        ],
        input_output_aliases={1 + n: n for n in range(len(earlier))},
        compiler_params=pltpu.CompilerParams(vmem_limit_bytes=24 << 20),
        cost_estimate=pl.CostEstimate(flops=10**7, bytes_accessed=2 << 20, transcendentals=0),
    )(parts, *earlier)


def on_device(queries, new_keys, new_values, cache_keys, cache_values, cached_len, span_order):
    requests, tokens, heads, dim = queries.shape

    def swapped(x, axis, flip=1):
        size = lax.axis_size(axis)
        return lax.ppermute(x, axis, [(n, n ^ flip) for n in range(size)])

    k_own = cache_keys.reshape(requests, -1, dim)
    v_own = cache_values.reshape(requests, -1, dim)
    n_own = jnp.stack(
        [new_keys.reshape(requests, -1, dim), new_values.reshape(requests, -1, dim)], 1
    )
    q_own = queries.reshape(requests, tokens * heads, dim)
    v_par = swapped(v_own, "core")
    q_other = swapped(q_own, "y")
    near = [swapped(q_own, "z", flip) for flip in (1, 3)]
    k_par = swapped(k_own, "core")
    n_par = swapped(n_own, "core")
    vt = prepare(cached_len, v_own, v_par)
    q_other, vt, near = lax.optimization_barrier((q_other, vt, near))
    next_to = [swapped(q_other, "z", flip) for flip in (1, 3)]
    far = swapped(jnp.stack([q_own, q_other]), "z", 2)

    common = (cached_len, span_order)
    keys = (k_own, k_par, n_own, n_par, vt)
    blocks = {(0, 0): 0, (0, 1): 1, (1, 0): 2, (3, 0): 3, (1, 1): 4, (3, 1): 5}
    arrays = [q_own, q_other, *near, *next_to, far]

    def tile(r, a, b):
        def half(place):
            return place + ((6, place[1]) if place[0] == 2 else (blocks[place], None))

        return (r, half(a), half(b))

    here, by_own, by_other, last = (
        ((0, 0), (0, 1)),
        ((1, 0), (3, 0)),
        ((1, 1), (3, 1)),
        ((2, 0), (2, 1)),
    )
    plan = (
        ((0, here), (0, by_own), (1, here)),
        ((0, by_other), (0, last)),
        ((1, by_own), (1, by_other), (1, last)),
    )
    plan = [tuple(tile(r, *pair) for r, pair in call) for call in plan]
    partials = attend(plan[0], *common, arrays[:4], *keys, [])
    received = []
    for r in range(requests):
        (parts,) = attend(plan[1 + r], *common, arrays, *keys, [partials[r]])
        sent = parts.reshape((64,) + parts.shape[3:])
        got = lax.all_to_all(sent, ("z", "y", "kv"), 0, 0, tiled=True)
        received.append(got.reshape((8, 8) + parts.shape[3:]))
    results = []
    for r in range(requests):
        results = combine(r, requests, received[r], results)
    attention, norm = results
    return attention.reshape(requests, tokens // 8, 8 * heads, dim), norm


def solution(mesh):
    split = Mesh(mesh.devices.reshape(2, 4, 2, 8), ("y", "z", "core", "kv"))
    ctx = ("y", "z", "core")
    placed = P(None, ctx, "kv", None)
    return jax.shard_map(
        on_device,
        mesh=split,
        in_specs=(placed,) * 5 + (P(), P()),
        out_specs=(
            P(None, ctx + ("kv",), None, None),
            P(None, ctx + ("kv",), None),
        ),
        check_vma=False,
    )
```

```python
import functools

import jax
import jax.numpy as jnp
from jax import lax
from jax.experimental import pallas as pl
from jax.experimental.pallas import tpu as pltpu
from jax.sharding import Mesh
from jax.sharding import PartitionSpec as P

LOG2E = 1.4426950408889634
LN2 = 0.6931471805599453
MASKED = -1e30
SUM_LOW = 2.0**-60
SUM_HIGH = 2.0**100
VMEM = 40 << 20
VMEM_ALL = 60 << 20


def dot_nt(a, b):
    return lax.dot_general(a, b, (((1,), (1,)), ((), ())), preferred_element_type=jnp.float32)


def my_place():
    y, z, core = lax.axis_index("y"), lax.axis_index("z"), lax.axis_index("core")
    return (y * 4 + z) * 2 + core, core, y, z, lax.axis_index("kv")


def prepare_kernel(len_ref, vo_ref, vp_ref, vt_ref):
    r = pl.program_id(0)
    rows = vo_ref.shape[1]
    extra = vt_ref.shape[1] - 128
    me, core = my_place()[:2]
    for part, ref in enumerate((vo_ref, vp_ref)):
        owner = me if part == 0 else me + 1 - 2 * core
        valid = len_ref[r] - owner * rows
        row_id = lax.broadcasted_iota(jnp.int32, (rows, 128), 0)
        kept = jnp.where(row_id < valid, ref[0].astype(jnp.float32), 0.0).astype(jnp.bfloat16)
        vt_ref[0, :128, part * rows : (part + 1) * rows] = jnp.transpose(kept)
        col_id = lax.broadcasted_iota(jnp.int32, (extra, rows), 1)
        vt_ref[0, 128:, part * rows : (part + 1) * rows] = jnp.where(
            col_id < valid, 1.0, 0.0
        ).astype(jnp.bfloat16)


def prepare(cached_len, v_own, v_par):
    requests, rows, dim = v_own.shape
    whole = pl.BlockSpec((1, rows, dim), lambda r, *_: (r, 0, 0))
    return pl.pallas_call(
        prepare_kernel,
        grid_spec=pltpu.PrefetchScalarGridSpec(
            num_scalar_prefetch=1,
            grid=(requests,),
            in_specs=[whole, whole],
            out_specs=pl.BlockSpec((1, 144, 2 * rows), lambda r, *_: (r, 0, 0)),
        ),
        out_shape=jax.ShapeDtypeStruct((requests, 144, 2 * rows), jnp.bfloat16),
        compiler_params=pltpu.CompilerParams(vmem_limit_bytes=VMEM),
        cost_estimate=pl.CostEstimate(flops=10**6, bytes_accessed=4 << 20, transcendentals=0),
    )(cached_len, v_own, v_par)


def attend_kernel(tiles, n_q, n_aliased, len_ref, span_ref, *refs):
    inputs = refs[: n_q + 5]
    n_out = 1 + max(tile[0] for tile in tiles) - min(tile[0] for tile in tiles)
    first_out = n_q + 5 + n_aliased
    out_refs = refs[first_out : first_out + n_out]
    scratch = refs[first_out + n_out :]
    ko_ref, kp_ref, no_ref, np_ref, vt_ref = scratch[:5]
    q_buf, acc_ref, top_ref, stage, sem, in_sem, q_sem = scratch[5:]
    requests = sorted({tile[0] for tile in tiles})
    lowest = requests[0]
    rows = ko_ref.shape[1]

    loads = {}

    def load(name, source, target):
        loads[name] = pltpu.make_async_copy(source, target, in_sem.at[len(loads)])
        loads[name].start()

    def fetch(request, t, half, source=0, part=None):
        array = inputs[source] if part is None else inputs[source].at[part]
        return pltpu.make_async_copy(array.at[request], q_buf.at[t, half], q_sem.at[2 * t + half])

    def load_q(t):
        for half in range(2):
            source, part = tiles[t][1 + half][2:]
            fetch(tiles[t][0], t, half, source, part).start()

    load_q(0)
    for r in requests:
        at = r - lowest
        load(("ko", 0, r), inputs[n_q].at[r], ko_ref.at[at])
        for n in range(2):
            part = pl.ds(n * rows, rows)
            load(("v", n, r), inputs[n_q + 4].at[r, :, part], vt_ref.at[at, :, part])
        load(("kp", 0, r), inputs[n_q + 1].at[r], kp_ref.at[at])
        load(("no", 0, r), inputs[n_q + 2].at[r], no_ref.at[at])
        load(("np", 0, r), inputs[n_q + 3].at[r], np_ref.at[at])
    for t in range(1, len(tiles)):
        load_q(t)
    me, core, my_y, my_z, _ = my_place()
    partner = me + 1 - 2 * core
    n_new = 2 * no_ref.shape[2]
    block = q_buf.shape[2]
    width = 2 * block
    scale = LOG2E * 128**-0.5

    def of_tile(t, choose):
        value = jnp.int32(choose(tiles[0]))
        for n in range(1, len(tiles)):
            value = jnp.where(t == n, jnp.int32(choose(tiles[n])), value)
        return value

    def request_of(t):
        return of_tile(t, lambda tile: tile[0])

    def new_visible(t):
        request = request_of(t)
        lane = lax.broadcasted_iota(jnp.int32, (1, width), 1)
        key = lax.broadcasted_iota(jnp.int32, (n_new, 1), 0)
        q_span = jnp.zeros((1, width), jnp.int32)
        k_span = jnp.zeros((n_new, 1), jnp.int32)
        first = jnp.int32(1 << 30)
        for n in range(4):
            hop_z = of_tile(t, lambda tile: tile[1 + n // 2][0])
            hop_y = of_tile(t, lambda tile: tile[1 + n // 2][1])
            source = 2 * ((my_y ^ hop_y) * 4 + (my_z ^ hop_z)) + core
            chosen = span_ref[request, 2 * source + n % 2]
            q_span = jnp.where(lane // (block // 2) == n, chosen, q_span)
            held = span_ref[request, 2 * (me if n < 2 else partner) + n % 2]
            k_span = jnp.where(key // 16 == n, held, k_span)
            first = jnp.minimum(first, held * 16)
        q_pos = q_span * 16 + lax.rem(lane // 16, 16)
        shown = (k_span * 16 + lax.rem(key, 16)) <= q_pos
        cached = len_ref[request] - jnp.minimum(me, partner) * rows > 0
        return shown, (q_pos >= first) | cached

    def values(request, p, start, size):
        return jnp.dot(
            vt_ref[request - lowest, :, pl.ds(start, size)],
            p.astype(jnp.bfloat16),
            preferred_element_type=jnp.float32,
        )

    def new_keys(at):
        return jnp.concatenate([no_ref[at, 0], np_ref[at, 0]], 0)

    def new_values(at, p):
        fresh = [no_ref[at, 1].astype(jnp.float32), np_ref[at, 1].astype(jnp.float32)]
        fresh = jnp.concatenate(fresh + [jnp.zeros((128 - n_new, 128), jnp.float32)], 0)
        turned = jnp.concatenate(
            [jnp.transpose(fresh), jnp.ones((vt_ref.shape[1] - 128, 128), jnp.float32)], 0
        ).astype(jnp.bfloat16)
        return jnp.dot(
            turned[:, :n_new], p.astype(jnp.bfloat16), preferred_element_type=jnp.float32
        )

    def sends(t, request):
        for half in range(2):
            hop_z, hop_y = (
                of_tile(t, lambda tile: tile[1 + half][axis]) for axis in range(2)
            )
            place = out_refs[request - lowest].at[my_z ^ hop_z, my_y ^ hop_y]
            yield pltpu.make_async_copy(stage.at[t, half], place, sem.at[2 * t + half])

    def start_sends(t):
        for r in requests:

            @pl.when(request_of(t) == r)
            def _(r=r):
                for copy in sends(t, r):
                    copy.start()

    def wait_for_sends():
        for t, tile in enumerate(tiles):
            for copy in sends(t, tile[0]):
                copy.wait()

    def finish(t, acc, top):
        total = acc[128:129, :]
        some = total > 0.0
        safe = jnp.where(some, total, 1.0)
        inverse = jnp.where(some, 1.0 / safe, 0.0)
        outputs = jnp.transpose(acc[:128, :] * inverse).astype(jnp.bfloat16)
        log_total = jnp.where(some, (top + jnp.log2(safe)) * LN2, MASKED)
        high = log_total.astype(jnp.bfloat16).astype(jnp.float32)
        middle = (log_total - high).astype(jnp.bfloat16).astype(jnp.float32)
        low = log_total - high - middle
        logs = jnp.concatenate(
            [high, middle, low, jnp.zeros((5, width), jnp.float32)], 0
        ).astype(jnp.bfloat16)
        owners = stage.shape[2]
        share = block // owners
        for n in range(2):
            stage[t, n, :, :share, :] = outputs[n * block : (n + 1) * block].reshape(
                owners, share, 128
            )
            for owner in range(owners):
                start = n * block + owner * share // 128 * 128
                stage[t, n, owner, share:, :] = logs[:, start : start + 128]

    def whole_tile(t, worst):
        request = request_of(t)
        at = request - lowest
        for r in requests:

            @pl.when(t == [tile[0] for tile in tiles].index(r))
            def _(r=r):
                for name, n in (("ko", 0), ("v", 0), ("kp", 0), ("v", 1), ("no", 0), ("np", 0)):
                    loads[name, n, r].wait()

        for half in range(2):
            fetch(0, t, half).wait()
        q = q_buf[t].reshape(width, 128)
        acc = values(request, jnp.exp2(dot_nt(ko_ref[at], q) * scale), 0, rows)
        acc = acc + values(request, jnp.exp2(dot_nt(kp_ref[at], q) * scale), rows, rows)
        shown, has_key = new_visible(t)
        s_new = jnp.where(shown, dot_nt(new_keys(at), q) * scale, MASKED)
        acc = acc + new_values(at, jnp.exp2(s_new))
        total = acc[128:129, :]
        fine = (total < SUM_HIGH) & ((total > SUM_LOW) | jnp.logical_not(has_key))
        finish(t, acc, jnp.zeros((1, width), jnp.float32))
        start_sends(t)
        return jnp.minimum(worst, jnp.where(fine, 1, 0))

    worst = lax.fori_loop(0, len(tiles), whole_tile, jnp.ones((1, width), jnp.int32))

    @pl.when(jnp.min(worst) == 0)
    def _():
        part = 256
        wait_for_sends()

        def again(t, carry):
            request = request_of(t)
            q = q_buf[t].reshape(width, 128)
            shown, _ = new_visible(t)
            s_new = jnp.where(shown, dot_nt(new_keys(request - lowest), q) * scale, MASKED)

            def highest(ref, valid, top):
                def body(j, top):
                    s = dot_nt(ref[request - lowest, pl.ds(j * part, part), :], q) * scale
                    row = lax.broadcasted_iota(jnp.int32, (part, width), 0) + j * part
                    s = jnp.where(row < valid, s, MASKED)
                    return jnp.maximum(top, jnp.max(s, 0, keepdims=True))

                return lax.fori_loop(0, rows // part, body, top)

            top = jnp.max(s_new, 0, keepdims=True)
            top = highest(ko_ref, len_ref[request] - me * rows, top)
            top = highest(kp_ref, len_ref[request] - partner * rows, top)
            p_new = jnp.where(shown, jnp.exp2(jnp.minimum(s_new - top, 0.0)), 0.0)
            acc_ref[...] = new_values(request - lowest, p_new)

            def add(ref, first):
                def body(j, carry):
                    s = dot_nt(ref[request - lowest, pl.ds(j * part, part), :], q) * scale
                    start = pl.multiple_of(first + j * part, part)
                    acc_ref[...] += values(
                        request, jnp.exp2(jnp.minimum(s - top, 0.0)), start, part
                    )
                    return carry

                lax.fori_loop(0, rows // part, body, 0)

            add(ko_ref, 0)
            add(kp_ref, rows)
            top_ref[...] = jnp.broadcast_to(top, top_ref.shape)
            finish(t, acc_ref[...], top_ref[0:1, :])
            start_sends(t)
            return carry

        lax.fori_loop(0, len(tiles), again, 0)

    wait_for_sends()


def attend(
    tiles, vmem, cached_len, span_order, q_arrays, k_own, k_par, n_own, n_par, vt, partials
):
    rows = k_own.shape[1]
    block = q_arrays[0].shape[-2]
    owners = 8
    share = block // owners
    width = 2 * block
    requests = sorted({tile[0] for tile in tiles})
    result = jax.ShapeDtypeStruct((4, 2, owners, share + 8, 128), jnp.bfloat16)
    keys = (k_own, k_par, n_own, n_par, vt)
    n_in = len(q_arrays) + len(keys)
    return pl.pallas_call(
        functools.partial(attend_kernel, tiles, len(q_arrays), len(partials)),
        in_specs=[pl.BlockSpec(memory_space=pltpu.SMEM)] * 2
        + [pl.BlockSpec(memory_space=pl.ANY)] * n_in
        + [pl.BlockSpec(memory_space=pltpu.HBM)] * len(partials),
        out_specs=[pl.BlockSpec(memory_space=pltpu.HBM)] * len(requests),
        scratch_shapes=[pltpu.VMEM((len(requests),) + x.shape[1:], x.dtype) for x in keys]
        + [
            pltpu.VMEM((len(tiles), 2, block, 128), jnp.bfloat16),
            pltpu.VMEM((144, width), jnp.float32),
            pltpu.VMEM((8, width), jnp.float32),
            pltpu.VMEM((len(tiles), 2, owners, share + 8, 128), jnp.bfloat16),
            pltpu.SemaphoreType.DMA((2 * len(tiles),)),
            pltpu.SemaphoreType.DMA((len(requests) * 6,)),
            pltpu.SemaphoreType.DMA((2 * len(tiles),)),
        ],
        out_shape=[result] * len(requests),
        input_output_aliases={2 + n_in + n: n for n in range(len(partials))},
        compiler_params=pltpu.CompilerParams(vmem_limit_bytes=vmem),
        cost_estimate=pl.CostEstimate(
            flops=len(tiles) * width * 2 * rows * 128 * 4,
            bytes_accessed=6 << 20,
            transcendentals=len(tiles) * width * 2 * rows,
        ),
    )(cached_len, span_order, *q_arrays, *keys, *partials)


def combine_kernel(request, in_ref, *refs):
    out_ref, norm_ref, held, sem = refs[-4:]
    sources, groups, rows, dim = held.shape
    share = rows - 8
    odd = lax.rem(lax.axis_index("kv"), 2) == 1
    copy = pltpu.make_async_copy(in_ref, held, sem)
    copy.start()
    lane = lax.broadcasted_iota(jnp.int32, (share, 128), 1)
    diagonal = lax.rem(lane, share) == lax.broadcasted_iota(jnp.int32, (share, 128), 0)
    shape = (sources, groups, 128)
    upper = lax.broadcasted_iota(jnp.int32, shape, 2) >= 64
    odd_source = lax.rem(lax.broadcasted_iota(jnp.int32, shape, 0), 2) == 1
    copy.wait()
    logs = held[:, :, share:, :].astype(jnp.float32)
    logs = logs[:, :, 0, :] + logs[:, :, 1, :] + logs[:, :, 2, :]
    turned = jnp.concatenate([logs[..., 64:], logs[..., :64]], 2)
    logs = jnp.where(upper == odd, logs, turned)
    highest = jnp.max(logs, 0)
    weight = jnp.exp(logs - highest[None])
    total = jnp.sum(weight, 0)
    norm = highest + jnp.log(total)
    shares = jnp.where(upper == odd_source, weight / total[None], 0.0)
    tokens = out_ref.shape[1]
    for group in range(groups):
        spread = jnp.concatenate(
            [
                jnp.where(
                    diagonal,
                    shares[n, group : group + 1] + shares[n + 1, group : group + 1],
                    0.0,
                )
                for n in range(0, sources, 2)
            ],
            1,
        )
        high = spread.astype(jnp.bfloat16)
        low = (spread - high.astype(jnp.float32)).astype(jnp.bfloat16)
        values = held[:, group, :share, :].reshape(sources * share, dim)
        summed = jnp.dot(high, values, preferred_element_type=jnp.float32) + jnp.dot(
            low, values, preferred_element_type=jnp.float32
        )
        out_ref[0, :, group] = summed.reshape(tokens, share // tokens, dim).astype(jnp.bfloat16)
    wide = share // tokens
    for token in range(tokens):
        norm_ref[0, token : token + 1, :] = jnp.concatenate(
            [norm[n : n + 1, token * wide : (token + 1) * wide] for n in range(groups)], 1
        )


def combine(request, requests, parts, earlier):
    sources, groups, rows, dim = parts.shape
    share = rows - 8
    tokens = share // 16
    shape = (requests, tokens, groups, 16, dim)
    return pl.pallas_call(
        functools.partial(combine_kernel, request),
        grid=(1,),
        in_specs=[pl.BlockSpec(memory_space=pl.ANY)] * (1 + len(earlier)),
        out_specs=[
            pl.BlockSpec((1,) + shape[1:], lambda *_: (request, 0, 0, 0, 0)),
            pl.BlockSpec((1, tokens, groups * 16), lambda *_: (request, 0, 0)),
        ],
        scratch_shapes=[
            pltpu.VMEM(parts.shape, parts.dtype),
            pltpu.SemaphoreType.DMA,
        ],
        out_shape=[
            jax.ShapeDtypeStruct(shape, jnp.bfloat16),
            jax.ShapeDtypeStruct((requests, tokens, groups * 16), jnp.float32),
        ],
        input_output_aliases={1 + n: n for n in range(len(earlier))},
        compiler_params=pltpu.CompilerParams(vmem_limit_bytes=24 << 20),
        cost_estimate=pl.CostEstimate(flops=10**7, bytes_accessed=2 << 20, transcendentals=0),
    )(parts, *earlier)


def on_device(queries, new_keys, new_values, cache_keys, cache_values, cached_len, span_order):
    requests, tokens, heads, dim = queries.shape

    def swapped(x, axis, flip=1):
        size = lax.axis_size(axis)
        return lax.ppermute(x, axis, [(n, n ^ flip) for n in range(size)])

    k_own = cache_keys.reshape(requests, -1, dim)
    v_own = cache_values.reshape(requests, -1, dim)
    n_own = jnp.stack(
        [new_keys.reshape(requests, -1, dim), new_values.reshape(requests, -1, dim)], 1
    )
    q_own = queries.reshape(requests, tokens * heads, dim)
    v_par = swapped(v_own, "core")
    q_other = swapped(q_own, "y")
    near = [swapped(q_own, "z", flip) for flip in (1, 3)]
    k_par = swapped(k_own, "core")
    n_par = swapped(n_own, "core")
    vt = prepare(cached_len, v_own, v_par)
    q_other, vt = lax.optimization_barrier((q_other, vt))
    next_to = [swapped(q_other, "z", flip) for flip in (1, 3)]
    q_both, near = lax.optimization_barrier((jnp.stack([q_own, q_other]), near))
    far = swapped(q_both, "z", 2)

    common = (cached_len, span_order)
    keys = (k_own, k_par, n_own, n_par, vt)
    blocks = {(0, 0): 0, (0, 1): 1, (1, 0): 2, (3, 0): 3, (1, 1): 4, (3, 1): 5}
    arrays = [q_own, q_other, *near, *next_to, far]

    def tile(r, a, b):
        def half(place):
            return place + ((6, place[1]) if place[0] == 2 else (blocks[place], None))

        return (r, half(a), half(b))

    here, by_own, by_other, last = (
        ((0, 0), (0, 1)),
        ((1, 0), (3, 0)),
        ((1, 1), (3, 1)),
        ((2, 0), (2, 1)),
    )
    plan = (
        ((0, here), (0, by_own), (1, here)),
        ((0, by_other), (0, last)),
        ((1, by_own), (1, by_other), (1, last)),
    )
    plan = [tuple(tile(r, *pair) for r, pair in call) for call in plan]
    partials = attend(plan[0], VMEM, *common, arrays[:4], *keys, [])
    received = []
    for r in range(requests):
        (parts,) = attend(plan[1 + r], VMEM if r == 0 else VMEM_ALL, *common, arrays, *keys, [partials[r]])
        sent = parts.reshape((64,) + parts.shape[3:])
        got = lax.all_to_all(sent, ("z", "y", "kv"), 0, 0, tiled=True)
        received.append(got.reshape((8, 8) + parts.shape[3:]))
    results = []
    for r in range(requests):
        results = combine(r, requests, received[r], results)
    attention, norm = results
    return attention.reshape(requests, tokens // 8, 8 * heads, dim), norm


def solution(mesh):
    split = Mesh(mesh.devices.reshape(2, 4, 2, 8), ("y", "z", "core", "kv"))
    ctx = ("y", "z", "core")
    placed = P(None, ctx, "kv", None)
    return jax.shard_map(
        on_device,
        mesh=split,
        in_specs=(placed,) * 5 + (P(), P()),
        out_specs=(
            P(None, ctx + ("kv",), None, None),
            P(None, ctx + ("kv",), None),
        ),
        check_vma=False,
    )
```

```python
import functools

import jax
import jax.numpy as jnp
from jax import lax
from jax.experimental import pallas as pl
from jax.experimental.pallas import tpu as pltpu
from jax.sharding import Mesh
from jax.sharding import PartitionSpec as P

LOG2E = 1.4426950408889634
LN2 = 0.6931471805599453
MASKED = -1e30
SUM_LOW = 2.0**-60
SUM_HIGH = 2.0**100
VMEM = 40 << 20
VMEM_ALL = 60 << 20


def dot_nt(a, b):
    return lax.dot_general(a, b, (((1,), (1,)), ((), ())), preferred_element_type=jnp.float32)


def my_place():
    y, z, core = lax.axis_index("y"), lax.axis_index("z"), lax.axis_index("core")
    return (y * 4 + z) * 2 + core, core, y, z, lax.axis_index("kv")


def prepare_kernel(len_ref, vo_ref, vp_ref, vt_ref):
    r = pl.program_id(0)
    rows = vo_ref.shape[1]
    extra = vt_ref.shape[1] - 128
    me, core = my_place()[:2]
    for part, ref in enumerate((vo_ref, vp_ref)):
        owner = me if part == 0 else me + 1 - 2 * core
        valid = len_ref[r] - owner * rows
        row_id = lax.broadcasted_iota(jnp.int32, (rows, 128), 0)
        kept = jnp.where(row_id < valid, ref[0].astype(jnp.float32), 0.0).astype(jnp.bfloat16)
        vt_ref[0, :128, part * rows : (part + 1) * rows] = jnp.transpose(kept)
        col_id = lax.broadcasted_iota(jnp.int32, (extra, rows), 1)
        vt_ref[0, 128:, part * rows : (part + 1) * rows] = jnp.where(
            col_id < valid, 1.0, 0.0
        ).astype(jnp.bfloat16)


def prepare(cached_len, v_own, v_par):
    requests, rows, dim = v_own.shape
    whole = pl.BlockSpec((1, rows, dim), lambda r, *_: (r, 0, 0))
    return pl.pallas_call(
        prepare_kernel,
        grid_spec=pltpu.PrefetchScalarGridSpec(
            num_scalar_prefetch=1,
            grid=(requests,),
            in_specs=[whole, whole],
            out_specs=pl.BlockSpec((1, 144, 2 * rows), lambda r, *_: (r, 0, 0)),
        ),
        out_shape=jax.ShapeDtypeStruct((requests, 144, 2 * rows), jnp.bfloat16),
        compiler_params=pltpu.CompilerParams(vmem_limit_bytes=VMEM),
        cost_estimate=pl.CostEstimate(flops=10**6, bytes_accessed=4 << 20, transcendentals=0),
    )(cached_len, v_own, v_par)


def attend_kernel(tiles, n_q, n_aliased, len_ref, span_ref, *refs):
    inputs = refs[: n_q + 5]
    n_out = 1 + max(tile[0] for tile in tiles) - min(tile[0] for tile in tiles)
    first_out = n_q + 5 + n_aliased
    out_refs = refs[first_out : first_out + n_out]
    scratch = refs[first_out + n_out :]
    ko_ref, kp_ref, no_ref, np_ref, vt_ref = scratch[:5]
    q_buf, acc_ref, top_ref, stage, sem, in_sem, q_sem = scratch[5:]
    requests = sorted({tile[0] for tile in tiles})
    lowest = requests[0]
    rows = ko_ref.shape[1]

    loads = {}

    def load(name, source, target):
        loads[name] = pltpu.make_async_copy(source, target, in_sem.at[len(loads)])
        loads[name].start()

    def fetch(request, t, half, source=0, part=None):
        array = inputs[source] if part is None else inputs[source].at[part]
        return pltpu.make_async_copy(array.at[request], q_buf.at[t, half], q_sem.at[2 * t + half])

    def load_q(t):
        for half in range(2):
            source, part = tiles[t][1 + half][2:]
            fetch(tiles[t][0], t, half, source, part).start()

    load_q(0)
    for r in requests:
        at = r - lowest
        load(("ko", 0, r), inputs[n_q].at[r], ko_ref.at[at])
        for n in range(2):
            part = pl.ds(n * rows, rows)
            load(("v", n, r), inputs[n_q + 4].at[r, :, part], vt_ref.at[at, :, part])
        load(("kp", 0, r), inputs[n_q + 1].at[r], kp_ref.at[at])
        load(("no", 0, r), inputs[n_q + 2].at[r], no_ref.at[at])
        load(("np", 0, r), inputs[n_q + 3].at[r], np_ref.at[at])
    for t in range(1, len(tiles)):
        load_q(t)
    me, core, my_y, my_z, _ = my_place()
    partner = me + 1 - 2 * core
    n_new = 2 * no_ref.shape[2]
    block = q_buf.shape[2]
    width = 2 * block
    scale = LOG2E * 128**-0.5

    def of_tile(t, choose):
        value = jnp.int32(choose(tiles[0]))
        for n in range(1, len(tiles)):
            value = jnp.where(t == n, jnp.int32(choose(tiles[n])), value)
        return value

    def request_of(t):
        return of_tile(t, lambda tile: tile[0])

    def new_visible(t):
        request = request_of(t)
        lane = lax.broadcasted_iota(jnp.int32, (1, width), 1)
        key = lax.broadcasted_iota(jnp.int32, (n_new, 1), 0)
        q_span = jnp.zeros((1, width), jnp.int32)
        k_span = jnp.zeros((n_new, 1), jnp.int32)
        first = jnp.int32(1 << 30)
        for n in range(4):
            hop_z = of_tile(t, lambda tile: tile[1 + n // 2][0])
            hop_y = of_tile(t, lambda tile: tile[1 + n // 2][1])
            source = 2 * ((my_y ^ hop_y) * 4 + (my_z ^ hop_z)) + core
            chosen = span_ref[request, 2 * source + n % 2]
            q_span = jnp.where(lane // (block // 2) == n, chosen, q_span)
            held = span_ref[request, 2 * (me if n < 2 else partner) + n % 2]
            k_span = jnp.where(key // 16 == n, held, k_span)
            first = jnp.minimum(first, held * 16)
        q_pos = q_span * 16 + lax.rem(lane // 16, 16)
        shown = (k_span * 16 + lax.rem(key, 16)) <= q_pos
        cached = len_ref[request] - jnp.minimum(me, partner) * rows > 0
        return shown, (q_pos >= first) | cached

    def values(request, p, start, size):
        return jnp.dot(
            vt_ref[request - lowest, :, pl.ds(start, size)],
            p.astype(jnp.bfloat16),
            preferred_element_type=jnp.float32,
        )

    def new_keys(at):
        return jnp.concatenate([no_ref[at, 0], np_ref[at, 0]], 0)

    def new_values(at, p):
        fresh = [no_ref[at, 1].astype(jnp.float32), np_ref[at, 1].astype(jnp.float32)]
        fresh = jnp.concatenate(fresh + [jnp.zeros((128 - n_new, 128), jnp.float32)], 0)
        turned = jnp.concatenate(
            [jnp.transpose(fresh), jnp.ones((vt_ref.shape[1] - 128, 128), jnp.float32)], 0
        ).astype(jnp.bfloat16)
        return jnp.dot(
            turned[:, :n_new], p.astype(jnp.bfloat16), preferred_element_type=jnp.float32
        )

    def sends(t, request):
        for half in range(2):
            hop_z, hop_y = (
                of_tile(t, lambda tile: tile[1 + half][axis]) for axis in range(2)
            )
            place = out_refs[request - lowest].at[my_z ^ hop_z ^ (2 * core), my_y ^ hop_y ^ core]
            yield pltpu.make_async_copy(stage.at[t, half], place, sem.at[2 * t + half])

    def start_sends(t):
        for r in requests:

            @pl.when(request_of(t) == r)
            def _(r=r):
                for copy in sends(t, r):
                    copy.start()

    def wait_for_sends():
        for t, tile in enumerate(tiles):
            for copy in sends(t, tile[0]):
                copy.wait()

    def finish(t, acc, top):
        total = acc[128:129, :]
        some = total > 0.0
        safe = jnp.where(some, total, 1.0)
        inverse = jnp.where(some, 1.0 / safe, 0.0)
        outputs = jnp.transpose(acc[:128, :] * inverse).astype(jnp.bfloat16)
        log_total = jnp.where(some, (top + jnp.log2(safe)) * LN2, MASKED)
        high = log_total.astype(jnp.bfloat16).astype(jnp.float32)
        middle = (log_total - high).astype(jnp.bfloat16).astype(jnp.float32)
        low = log_total - high - middle
        logs = jnp.concatenate(
            [high, middle, low, jnp.zeros((5, width), jnp.float32)], 0
        ).astype(jnp.bfloat16)
        owners = stage.shape[2]
        share = block // owners
        for n in range(2):
            stage[t, n, :, :share, :] = outputs[n * block : (n + 1) * block].reshape(
                owners, share, 128
            )
            for owner in range(owners):
                start = n * block + owner * share // 128 * 128
                stage[t, n, owner, share:, :] = logs[:, start : start + 128]

    def whole_tile(t, worst):
        request = request_of(t)
        at = request - lowest
        for r in requests:

            @pl.when(t == [tile[0] for tile in tiles].index(r))
            def _(r=r):
                for name, n in (("ko", 0), ("v", 0), ("kp", 0), ("v", 1), ("no", 0), ("np", 0)):
                    loads[name, n, r].wait()

        for half in range(2):
            fetch(0, t, half).wait()
        q = q_buf[t].reshape(width, 128)
        acc = values(request, jnp.exp2(dot_nt(ko_ref[at], q) * scale), 0, rows)
        acc = acc + values(request, jnp.exp2(dot_nt(kp_ref[at], q) * scale), rows, rows)
        shown, has_key = new_visible(t)
        s_new = jnp.where(shown, dot_nt(new_keys(at), q) * scale, MASKED)
        acc = acc + new_values(at, jnp.exp2(s_new))
        total = acc[128:129, :]
        fine = (total < SUM_HIGH) & ((total > SUM_LOW) | jnp.logical_not(has_key))
        finish(t, acc, jnp.zeros((1, width), jnp.float32))
        start_sends(t)
        return jnp.minimum(worst, jnp.where(fine, 1, 0))

    worst = lax.fori_loop(0, len(tiles), whole_tile, jnp.ones((1, width), jnp.int32))

    @pl.when(jnp.min(worst) == 0)
    def _():
        part = 256
        wait_for_sends()

        def again(t, carry):
            request = request_of(t)
            q = q_buf[t].reshape(width, 128)
            shown, _ = new_visible(t)
            s_new = jnp.where(shown, dot_nt(new_keys(request - lowest), q) * scale, MASKED)

            def highest(ref, valid, top):
                def body(j, top):
                    s = dot_nt(ref[request - lowest, pl.ds(j * part, part), :], q) * scale
                    row = lax.broadcasted_iota(jnp.int32, (part, width), 0) + j * part
                    s = jnp.where(row < valid, s, MASKED)
                    return jnp.maximum(top, jnp.max(s, 0, keepdims=True))

                return lax.fori_loop(0, rows // part, body, top)

            top = jnp.max(s_new, 0, keepdims=True)
            top = highest(ko_ref, len_ref[request] - me * rows, top)
            top = highest(kp_ref, len_ref[request] - partner * rows, top)
            p_new = jnp.where(shown, jnp.exp2(jnp.minimum(s_new - top, 0.0)), 0.0)
            acc_ref[...] = new_values(request - lowest, p_new)

            def add(ref, first):
                def body(j, carry):
                    s = dot_nt(ref[request - lowest, pl.ds(j * part, part), :], q) * scale
                    start = pl.multiple_of(first + j * part, part)
                    acc_ref[...] += values(
                        request, jnp.exp2(jnp.minimum(s - top, 0.0)), start, part
                    )
                    return carry

                lax.fori_loop(0, rows // part, body, 0)

            add(ko_ref, 0)
            add(kp_ref, rows)
            top_ref[...] = jnp.broadcast_to(top, top_ref.shape)
            finish(t, acc_ref[...], top_ref[0:1, :])
            start_sends(t)
            return carry

        lax.fori_loop(0, len(tiles), again, 0)

    wait_for_sends()


def attend(
    tiles, vmem, cached_len, span_order, q_arrays, k_own, k_par, n_own, n_par, vt, partials
):
    rows = k_own.shape[1]
    block = q_arrays[0].shape[-2]
    owners = 8
    share = block // owners
    width = 2 * block
    requests = sorted({tile[0] for tile in tiles})
    result = jax.ShapeDtypeStruct((4, 2, owners, share + 8, 128), jnp.bfloat16)
    keys = (k_own, k_par, n_own, n_par, vt)
    n_in = len(q_arrays) + len(keys)
    return pl.pallas_call(
        functools.partial(attend_kernel, tiles, len(q_arrays), len(partials)),
        in_specs=[pl.BlockSpec(memory_space=pltpu.SMEM)] * 2
        + [pl.BlockSpec(memory_space=pl.ANY)] * n_in
        + [pl.BlockSpec(memory_space=pltpu.HBM)] * len(partials),
        out_specs=[pl.BlockSpec(memory_space=pltpu.HBM)] * len(requests),
        scratch_shapes=[pltpu.VMEM((len(requests),) + x.shape[1:], x.dtype) for x in keys]
        + [
            pltpu.VMEM((len(tiles), 2, block, 128), jnp.bfloat16),
            pltpu.VMEM((144, width), jnp.float32),
            pltpu.VMEM((8, width), jnp.float32),
            pltpu.VMEM((len(tiles), 2, owners, share + 8, 128), jnp.bfloat16),
            pltpu.SemaphoreType.DMA((2 * len(tiles),)),
            pltpu.SemaphoreType.DMA((len(requests) * 6,)),
            pltpu.SemaphoreType.DMA((2 * len(tiles),)),
        ],
        out_shape=[result] * len(requests),
        input_output_aliases={2 + n_in + n: n for n in range(len(partials))},
        compiler_params=pltpu.CompilerParams(vmem_limit_bytes=vmem),
        cost_estimate=pl.CostEstimate(
            flops=len(tiles) * width * 2 * rows * 128 * 4,
            bytes_accessed=6 << 20,
            transcendentals=len(tiles) * width * 2 * rows,
        ),
    )(cached_len, span_order, *q_arrays, *keys, *partials)


def combine_kernel(request, in_ref, *refs):
    out_ref, norm_ref, held, sem = refs[-4:]
    sources, groups, rows, dim = held.shape
    share = rows - 8
    odd = lax.rem(lax.axis_index("kv"), 2) == 1
    copy = pltpu.make_async_copy(in_ref, held, sem)
    copy.start()
    lane = lax.broadcasted_iota(jnp.int32, (share, 128), 1)
    diagonal = lax.rem(lane, share) == lax.broadcasted_iota(jnp.int32, (share, 128), 0)
    shape = (sources, groups, 128)
    upper = lax.broadcasted_iota(jnp.int32, shape, 2) >= 64
    odd_source = lax.rem(lax.broadcasted_iota(jnp.int32, shape, 0), 2) == 1
    copy.wait()
    logs = held[:, :, share:, :].astype(jnp.float32)
    logs = logs[:, :, 0, :] + logs[:, :, 1, :] + logs[:, :, 2, :]
    turned = jnp.concatenate([logs[..., 64:], logs[..., :64]], 2)
    logs = jnp.where(upper == odd, logs, turned)
    highest = jnp.max(logs, 0)
    weight = jnp.exp(logs - highest[None])
    total = jnp.sum(weight, 0)
    norm = highest + jnp.log(total)
    shares = jnp.where(upper == odd_source, weight / total[None], 0.0)
    tokens = out_ref.shape[1]
    for group in range(groups):
        spread = jnp.concatenate(
            [
                jnp.where(
                    diagonal,
                    shares[n, group : group + 1] + shares[n + 1, group : group + 1],
                    0.0,
                )
                for n in range(0, sources, 2)
            ],
            1,
        )
        high = spread.astype(jnp.bfloat16)
        low = (spread - high.astype(jnp.float32)).astype(jnp.bfloat16)
        values = held[:, group, :share, :].reshape(sources * share, dim)
        summed = jnp.dot(high, values, preferred_element_type=jnp.float32) + jnp.dot(
            low, values, preferred_element_type=jnp.float32
        )
        out_ref[0, :, group] = summed.reshape(tokens, share // tokens, dim).astype(jnp.bfloat16)
    wide = share // tokens
    for token in range(tokens):
        norm_ref[0, token : token + 1, :] = jnp.concatenate(
            [norm[n : n + 1, token * wide : (token + 1) * wide] for n in range(groups)], 1
        )


def combine(request, requests, parts, earlier):
    sources, groups, rows, dim = parts.shape
    share = rows - 8
    tokens = share // 16
    shape = (requests, tokens, groups, 16, dim)
    return pl.pallas_call(
        functools.partial(combine_kernel, request),
        grid=(1,),
        in_specs=[pl.BlockSpec(memory_space=pl.ANY)] * (1 + len(earlier)),
        out_specs=[
            pl.BlockSpec((1,) + shape[1:], lambda *_: (request, 0, 0, 0, 0)),
            pl.BlockSpec((1, tokens, groups * 16), lambda *_: (request, 0, 0)),
        ],
        scratch_shapes=[
            pltpu.VMEM(parts.shape, parts.dtype),
            pltpu.SemaphoreType.DMA,
        ],
        out_shape=[
            jax.ShapeDtypeStruct(shape, jnp.bfloat16),
            jax.ShapeDtypeStruct((requests, tokens, groups * 16), jnp.float32),
        ],
        input_output_aliases={1 + n: n for n in range(len(earlier))},
        compiler_params=pltpu.CompilerParams(vmem_limit_bytes=24 << 20),
        cost_estimate=pl.CostEstimate(flops=10**7, bytes_accessed=2 << 20, transcendentals=0),
    )(parts, *earlier)


def on_device(queries, new_keys, new_values, cache_keys, cache_values, cached_len, span_order):
    requests, tokens, heads, dim = queries.shape

    def swapped(x, axis, flip=1):
        size = lax.axis_size(axis)
        return lax.ppermute(x, axis, [(n, n ^ flip) for n in range(size)])

    k_own = cache_keys.reshape(requests, -1, dim)
    v_own = cache_values.reshape(requests, -1, dim)
    n_own = jnp.stack(
        [new_keys.reshape(requests, -1, dim), new_values.reshape(requests, -1, dim)], 1
    )
    q_own = queries.reshape(requests, tokens * heads, dim)
    v_par = swapped(v_own, "core")
    q_other = swapped(q_own, "y")
    near = [swapped(q_own, "z", flip) for flip in (1, 3)]
    k_par = swapped(k_own, "core")
    n_par = swapped(n_own, "core")
    vt = prepare(cached_len, v_own, v_par)
    q_other, vt = lax.optimization_barrier((q_other, vt))
    next_to = [swapped(q_other, "z", flip) for flip in (1, 3)]
    q_both, near = lax.optimization_barrier((jnp.stack([q_own, q_other]), near))
    far = swapped(q_both, "z", 2)

    common = (cached_len, span_order)
    keys = (k_own, k_par, n_own, n_par, vt)
    blocks = {(0, 0): 0, (0, 1): 1, (1, 0): 2, (3, 0): 3, (1, 1): 4, (3, 1): 5}
    arrays = [q_own, q_other, *near, *next_to, far]

    def tile(r, a, b):
        def half(place):
            return place + ((6, place[1]) if place[0] == 2 else (blocks[place], None))

        return (r, half(a), half(b))

    here, by_own, by_other, last = (
        ((0, 0), (0, 1)),
        ((1, 0), (3, 0)),
        ((1, 1), (3, 1)),
        ((2, 0), (2, 1)),
    )
    plan = (
        ((0, here), (0, by_own), (1, here)),
        ((0, by_other), (0, last)),
        ((1, by_own), (1, by_other), (1, last)),
    )
    plan = [tuple(tile(r, *pair) for r, pair in call) for call in plan]
    partials = attend(plan[0], VMEM, *common, arrays[:4], *keys, [])
    groups = [
        [
            (((y ^ core) * 4 + (z ^ (2 * core))) * 2 + core) * 8 + kv
            for z in range(4)
            for y in range(2)
            for kv in range(8)
        ]
        for core in range(2)
    ]
    received = []
    for r in range(requests):
        (parts,) = attend(plan[1 + r], VMEM if r == 0 else VMEM_ALL, *common, arrays, *keys, [partials[r]])
        sent = parts.reshape((64,) + parts.shape[3:])
        got = lax.all_to_all(
            sent, ("y", "z", "core", "kv"), 0, 0, axis_index_groups=groups, tiled=True
        )
        received.append(got.reshape((8, 8) + parts.shape[3:]))
    results = []
    for r in range(requests):
        results = combine(r, requests, received[r], results)
    attention, norm = results
    return attention.reshape(requests, tokens // 8, 8 * heads, dim), norm


def solution(mesh):
    split = Mesh(mesh.devices.reshape(2, 4, 2, 8), ("y", "z", "core", "kv"))
    ctx = ("y", "z", "core")
    placed = P(None, ctx, "kv", None)
    return jax.shard_map(
        on_device,
        mesh=split,
        in_specs=(placed,) * 5 + (P(), P()),
        out_specs=(
            P(None, ctx + ("kv",), None, None),
            P(None, ctx + ("kv",), None),
        ),
        check_vma=False,
    )
```

```python
import functools

import jax
import jax.numpy as jnp
from jax import lax
from jax.experimental import pallas as pl
from jax.experimental.pallas import tpu as pltpu
from jax.sharding import Mesh
from jax.sharding import PartitionSpec as P

LOG2E = 1.4426950408889634
LN2 = 0.6931471805599453
MASKED = -1e30
SUM_LOW = 2.0**-60
SUM_HIGH = 2.0**100
VMEM = 40 << 20
VMEM_ALL = 60 << 20


def dot_nt(a, b):
    return lax.dot_general(a, b, (((1,), (1,)), ((), ())), preferred_element_type=jnp.float32)


def my_place():
    y, z, core = lax.axis_index("y"), lax.axis_index("z"), lax.axis_index("core")
    return (y * 4 + z) * 2 + core, core, y, z, lax.axis_index("kv")


def prepare_kernel(len_ref, vo_ref, vp_ref, vt_ref):
    r = pl.program_id(0)
    rows = vo_ref.shape[1]
    extra = vt_ref.shape[1] - 128
    me, core = my_place()[:2]
    for part, ref in enumerate((vo_ref, vp_ref)):
        owner = me if part == 0 else me + 1 - 2 * core
        valid = len_ref[r] - owner * rows
        row_id = lax.broadcasted_iota(jnp.int32, (rows, 128), 0)
        kept = jnp.where(row_id < valid, ref[0].astype(jnp.float32), 0.0).astype(jnp.bfloat16)
        vt_ref[0, :128, part * rows : (part + 1) * rows] = jnp.transpose(kept)
        col_id = lax.broadcasted_iota(jnp.int32, (extra, rows), 1)
        vt_ref[0, 128:, part * rows : (part + 1) * rows] = jnp.where(
            col_id < valid, 1.0, 0.0
        ).astype(jnp.bfloat16)


def prepare(cached_len, v_own, v_par):
    requests, rows, dim = v_own.shape
    whole = pl.BlockSpec((1, rows, dim), lambda r, *_: (r, 0, 0))
    return pl.pallas_call(
        prepare_kernel,
        grid_spec=pltpu.PrefetchScalarGridSpec(
            num_scalar_prefetch=1,
            grid=(requests,),
            in_specs=[whole, whole],
            out_specs=pl.BlockSpec((1, 144, 2 * rows), lambda r, *_: (r, 0, 0)),
        ),
        out_shape=jax.ShapeDtypeStruct((requests, 144, 2 * rows), jnp.bfloat16),
        compiler_params=pltpu.CompilerParams(vmem_limit_bytes=VMEM),
        cost_estimate=pl.CostEstimate(flops=10**6, bytes_accessed=4 << 20, transcendentals=0),
    )(cached_len, v_own, v_par)


def attend_kernel(tiles, n_q, carried, len_ref, span_ref, *refs):
    inputs = refs[: n_q + 5]
    n_out = 1 + max(tile[0] for tile in tiles) - min(tile[0] for tile in tiles)
    first_out = n_q + 5 + (1 if carried else 0)
    out_refs = refs[first_out : first_out + n_out]
    scratch = refs[first_out + n_out :]
    ko_ref, kp_ref, no_ref, np_ref, vt_ref = scratch[:5]
    q_buf, acc_ref, top_ref, stage, sem, in_sem, q_sem, carry_sem = scratch[5:]
    requests = sorted({tile[0] for tile in tiles})
    lowest = requests[0]
    rows = ko_ref.shape[1]

    loads = {}

    def load(name, source, target):
        loads[name] = pltpu.make_async_copy(source, target, in_sem.at[len(loads)])
        loads[name].start()

    def fetch(request, t, half, source=0, part=None):
        array = inputs[source] if part is None else inputs[source].at[part]
        return pltpu.make_async_copy(array.at[request], q_buf.at[t, half], q_sem.at[2 * t + half])

    def load_q(t):
        for half in range(2):
            source, part = tiles[t][1 + half][2:]
            fetch(tiles[t][0], t, half, source, part).start()

    load_q(0)
    for r in requests:
        at = r - lowest
        load(("ko", 0, r), inputs[n_q].at[r], ko_ref.at[at])
        for n in range(2):
            part = pl.ds(n * rows, rows)
            load(("v", n, r), inputs[n_q + 4].at[r, :, part], vt_ref.at[at, :, part])
        load(("kp", 0, r), inputs[n_q + 1].at[r], kp_ref.at[at])
        load(("no", 0, r), inputs[n_q + 2].at[r], no_ref.at[at])
        load(("np", 0, r), inputs[n_q + 3].at[r], np_ref.at[at])
    for t in range(1, len(tiles)):
        load_q(t)
    me, core, my_y, my_z, _ = my_place()
    partner = me + 1 - 2 * core

    def carries():
        for n, (hop_z, hop_y) in enumerate(carried):
            place = (my_z ^ hop_z ^ (2 * core), my_y ^ hop_y ^ core)
            yield pltpu.make_async_copy(
                refs[n_q + 5].at[place], out_refs[0].at[place], carry_sem.at[n]
            )

    for copy in carries():
        copy.start()
    n_new = 2 * no_ref.shape[2]
    block = q_buf.shape[2]
    width = 2 * block
    scale = LOG2E * 128**-0.5

    def of_tile(t, choose):
        value = jnp.int32(choose(tiles[0]))
        for n in range(1, len(tiles)):
            value = jnp.where(t == n, jnp.int32(choose(tiles[n])), value)
        return value

    def request_of(t):
        return of_tile(t, lambda tile: tile[0])

    def new_visible(t):
        request = request_of(t)
        lane = lax.broadcasted_iota(jnp.int32, (1, width), 1)
        key = lax.broadcasted_iota(jnp.int32, (n_new, 1), 0)
        q_span = jnp.zeros((1, width), jnp.int32)
        k_span = jnp.zeros((n_new, 1), jnp.int32)
        first = jnp.int32(1 << 30)
        for n in range(4):
            hop_z = of_tile(t, lambda tile: tile[1 + n // 2][0])
            hop_y = of_tile(t, lambda tile: tile[1 + n // 2][1])
            source = 2 * ((my_y ^ hop_y) * 4 + (my_z ^ hop_z)) + core
            chosen = span_ref[request, 2 * source + n % 2]
            q_span = jnp.where(lane // (block // 2) == n, chosen, q_span)
            held = span_ref[request, 2 * (me if n < 2 else partner) + n % 2]
            k_span = jnp.where(key // 16 == n, held, k_span)
            first = jnp.minimum(first, held * 16)
        q_pos = q_span * 16 + lax.rem(lane // 16, 16)
        shown = (k_span * 16 + lax.rem(key, 16)) <= q_pos
        cached = len_ref[request] - jnp.minimum(me, partner) * rows > 0
        return shown, (q_pos >= first) | cached

    def values(request, p, start, size):
        return jnp.dot(
            vt_ref[request - lowest, :, pl.ds(start, size)],
            p.astype(jnp.bfloat16),
            preferred_element_type=jnp.float32,
        )

    def new_keys(at):
        return jnp.concatenate([no_ref[at, 0], np_ref[at, 0]], 0)

    def new_values(at, p):
        fresh = [no_ref[at, 1].astype(jnp.float32), np_ref[at, 1].astype(jnp.float32)]
        fresh = jnp.concatenate(fresh + [jnp.zeros((128 - n_new, 128), jnp.float32)], 0)
        turned = jnp.concatenate(
            [jnp.transpose(fresh), jnp.ones((vt_ref.shape[1] - 128, 128), jnp.float32)], 0
        ).astype(jnp.bfloat16)
        return jnp.dot(
            turned[:, :n_new], p.astype(jnp.bfloat16), preferred_element_type=jnp.float32
        )

    def sends(t, request):
        for half in range(2):
            hop_z, hop_y = (
                of_tile(t, lambda tile: tile[1 + half][axis]) for axis in range(2)
            )
            place = out_refs[request - lowest].at[my_z ^ hop_z ^ (2 * core), my_y ^ hop_y ^ core]
            yield pltpu.make_async_copy(stage.at[t, half], place, sem.at[2 * t + half])

    def start_sends(t):
        for r in requests:

            @pl.when(request_of(t) == r)
            def _(r=r):
                for copy in sends(t, r):
                    copy.start()

    def wait_for_sends():
        for t, tile in enumerate(tiles):
            for copy in sends(t, tile[0]):
                copy.wait()

    def finish(t, acc, top):
        total = acc[128:129, :]
        some = total > 0.0
        safe = jnp.where(some, total, 1.0)
        inverse = jnp.where(some, 1.0 / safe, 0.0)
        outputs = jnp.transpose(acc[:128, :] * inverse).astype(jnp.bfloat16)
        log_total = jnp.where(some, (top + jnp.log2(safe)) * LN2, MASKED)
        high = log_total.astype(jnp.bfloat16).astype(jnp.float32)
        middle = (log_total - high).astype(jnp.bfloat16).astype(jnp.float32)
        low = log_total - high - middle
        logs = jnp.concatenate(
            [high, middle, low, jnp.zeros((5, width), jnp.float32)], 0
        ).astype(jnp.bfloat16)
        owners = stage.shape[2]
        share = block // owners
        for n in range(2):
            stage[t, n, :, :share, :] = outputs[n * block : (n + 1) * block].reshape(
                owners, share, 128
            )
            for owner in range(owners):
                start = n * block + owner * share // 128 * 128
                stage[t, n, owner, share:, :] = logs[:, start : start + 128]

    def whole_tile(t, worst):
        request = request_of(t)
        at = request - lowest
        for r in requests:

            @pl.when(t == [tile[0] for tile in tiles].index(r))
            def _(r=r):
                for name, n in (("ko", 0), ("v", 0), ("kp", 0), ("v", 1), ("no", 0), ("np", 0)):
                    loads[name, n, r].wait()

        for half in range(2):
            fetch(0, t, half).wait()
        q = q_buf[t].reshape(width, 128)
        acc = values(request, jnp.exp2(dot_nt(ko_ref[at], q) * scale), 0, rows)
        acc = acc + values(request, jnp.exp2(dot_nt(kp_ref[at], q) * scale), rows, rows)
        shown, has_key = new_visible(t)
        s_new = jnp.where(shown, dot_nt(new_keys(at), q) * scale, MASKED)
        acc = acc + new_values(at, jnp.exp2(s_new))
        total = acc[128:129, :]
        fine = (total < SUM_HIGH) & ((total > SUM_LOW) | jnp.logical_not(has_key))
        finish(t, acc, jnp.zeros((1, width), jnp.float32))
        start_sends(t)
        return jnp.minimum(worst, jnp.where(fine, 1, 0))

    worst = lax.fori_loop(0, len(tiles), whole_tile, jnp.ones((1, width), jnp.int32))

    @pl.when(jnp.min(worst) == 0)
    def _():
        part = 256
        wait_for_sends()

        def again(t, carry):
            request = request_of(t)
            q = q_buf[t].reshape(width, 128)
            shown, _ = new_visible(t)
            s_new = jnp.where(shown, dot_nt(new_keys(request - lowest), q) * scale, MASKED)

            def highest(ref, valid, top):
                def body(j, top):
                    s = dot_nt(ref[request - lowest, pl.ds(j * part, part), :], q) * scale
                    row = lax.broadcasted_iota(jnp.int32, (part, width), 0) + j * part
                    s = jnp.where(row < valid, s, MASKED)
                    return jnp.maximum(top, jnp.max(s, 0, keepdims=True))

                return lax.fori_loop(0, rows // part, body, top)

            top = jnp.max(s_new, 0, keepdims=True)
            top = highest(ko_ref, len_ref[request] - me * rows, top)
            top = highest(kp_ref, len_ref[request] - partner * rows, top)
            p_new = jnp.where(shown, jnp.exp2(jnp.minimum(s_new - top, 0.0)), 0.0)
            acc_ref[...] = new_values(request - lowest, p_new)

            def add(ref, first):
                def body(j, carry):
                    s = dot_nt(ref[request - lowest, pl.ds(j * part, part), :], q) * scale
                    start = pl.multiple_of(first + j * part, part)
                    acc_ref[...] += values(
                        request, jnp.exp2(jnp.minimum(s - top, 0.0)), start, part
                    )
                    return carry

                lax.fori_loop(0, rows // part, body, 0)

            add(ko_ref, 0)
            add(kp_ref, rows)
            top_ref[...] = jnp.broadcast_to(top, top_ref.shape)
            finish(t, acc_ref[...], top_ref[0:1, :])
            start_sends(t)
            return carry

        lax.fori_loop(0, len(tiles), again, 0)

    wait_for_sends()
    for copy in carries():
        copy.wait()


def attend(
    tiles, vmem, cached_len, span_order, q_arrays, k_own, k_par, n_own, n_par, vt, partial, carried
):
    rows = k_own.shape[1]
    block = q_arrays[0].shape[-2]
    owners = 8
    share = block // owners
    width = 2 * block
    requests = sorted({tile[0] for tile in tiles})
    result = jax.ShapeDtypeStruct((4, 2, owners, share + 8, 128), jnp.bfloat16)
    keys = (k_own, k_par, n_own, n_par, vt)
    n_in = len(q_arrays) + len(keys)
    return pl.pallas_call(
        functools.partial(attend_kernel, tiles, len(q_arrays), carried),
        in_specs=[pl.BlockSpec(memory_space=pltpu.SMEM)] * 2
        + [pl.BlockSpec(memory_space=pl.ANY)] * (n_in + len(partial)),
        out_specs=[pl.BlockSpec(memory_space=pltpu.HBM)] * len(requests),
        scratch_shapes=[pltpu.VMEM((len(requests),) + x.shape[1:], x.dtype) for x in keys]
        + [
            pltpu.VMEM((len(tiles), 2, block, 128), jnp.bfloat16),
            pltpu.VMEM((144, width), jnp.float32),
            pltpu.VMEM((8, width), jnp.float32),
            pltpu.VMEM((len(tiles), 2, owners, share + 8, 128), jnp.bfloat16),
            pltpu.SemaphoreType.DMA((2 * len(tiles),)),
            pltpu.SemaphoreType.DMA((len(requests) * 6,)),
            pltpu.SemaphoreType.DMA((2 * len(tiles),)),
            pltpu.SemaphoreType.DMA((max(1, len(carried)),)),
        ],
        out_shape=[result] * len(requests),
        compiler_params=pltpu.CompilerParams(vmem_limit_bytes=vmem),
        cost_estimate=pl.CostEstimate(
            flops=len(tiles) * width * 2 * rows * 128 * 4,
            bytes_accessed=6 << 20,
            transcendentals=len(tiles) * width * 2 * rows,
        ),
    )(cached_len, span_order, *q_arrays, *keys, *partial)


def combine_kernel(request, in_ref, *refs):
    out_ref, norm_ref, held, sem = refs[-4:]
    sources, groups, rows, dim = held.shape
    share = rows - 8
    odd = lax.rem(lax.axis_index("kv"), 2) == 1
    copy = pltpu.make_async_copy(in_ref, held, sem)
    copy.start()
    lane = lax.broadcasted_iota(jnp.int32, (share, 128), 1)
    diagonal = lax.rem(lane, share) == lax.broadcasted_iota(jnp.int32, (share, 128), 0)
    shape = (sources, groups, 128)
    upper = lax.broadcasted_iota(jnp.int32, shape, 2) >= 64
    odd_source = lax.rem(lax.broadcasted_iota(jnp.int32, shape, 0), 2) == 1
    copy.wait()
    logs = held[:, :, share:, :].astype(jnp.float32)
    logs = logs[:, :, 0, :] + logs[:, :, 1, :] + logs[:, :, 2, :]
    turned = jnp.concatenate([logs[..., 64:], logs[..., :64]], 2)
    logs = jnp.where(upper == odd, logs, turned)
    highest = jnp.max(logs, 0)
    weight = jnp.exp(logs - highest[None])
    total = jnp.sum(weight, 0)
    norm = highest + jnp.log(total)
    shares = jnp.where(upper == odd_source, weight / total[None], 0.0)
    tokens = out_ref.shape[1]
    for group in range(groups):
        spread = jnp.concatenate(
            [
                jnp.where(
                    diagonal,
                    shares[n, group : group + 1] + shares[n + 1, group : group + 1],
                    0.0,
                )
                for n in range(0, sources, 2)
            ],
            1,
        )
        high = spread.astype(jnp.bfloat16)
        low = (spread - high.astype(jnp.float32)).astype(jnp.bfloat16)
        values = held[:, group, :share, :].reshape(sources * share, dim)
        summed = jnp.dot(high, values, preferred_element_type=jnp.float32) + jnp.dot(
            low, values, preferred_element_type=jnp.float32
        )
        out_ref[0, :, group] = summed.reshape(tokens, share // tokens, dim).astype(jnp.bfloat16)
    wide = share // tokens
    for token in range(tokens):
        norm_ref[0, token : token + 1, :] = jnp.concatenate(
            [norm[n : n + 1, token * wide : (token + 1) * wide] for n in range(groups)], 1
        )


def combine(request, requests, parts, earlier):
    sources, groups, rows, dim = parts.shape
    share = rows - 8
    tokens = share // 16
    shape = (requests, tokens, groups, 16, dim)
    return pl.pallas_call(
        functools.partial(combine_kernel, request),
        grid=(1,),
        in_specs=[pl.BlockSpec(memory_space=pl.ANY)] * (1 + len(earlier)),
        out_specs=[
            pl.BlockSpec((1,) + shape[1:], lambda *_: (request, 0, 0, 0, 0)),
            pl.BlockSpec((1, tokens, groups * 16), lambda *_: (request, 0, 0)),
        ],
        scratch_shapes=[
            pltpu.VMEM(parts.shape, parts.dtype),
            pltpu.SemaphoreType.DMA,
        ],
        out_shape=[
            jax.ShapeDtypeStruct(shape, jnp.bfloat16),
            jax.ShapeDtypeStruct((requests, tokens, groups * 16), jnp.float32),
        ],
        input_output_aliases={1 + n: n for n in range(len(earlier))},
        compiler_params=pltpu.CompilerParams(vmem_limit_bytes=24 << 20),
        cost_estimate=pl.CostEstimate(flops=10**7, bytes_accessed=2 << 20, transcendentals=0),
    )(parts, *earlier)


def on_device(queries, new_keys, new_values, cache_keys, cache_values, cached_len, span_order):
    requests, tokens, heads, dim = queries.shape

    def swapped(x, axis, flip=1):
        size = lax.axis_size(axis)
        return lax.ppermute(x, axis, [(n, n ^ flip) for n in range(size)])

    k_own = cache_keys.reshape(requests, -1, dim)
    v_own = cache_values.reshape(requests, -1, dim)
    n_own = jnp.stack(
        [new_keys.reshape(requests, -1, dim), new_values.reshape(requests, -1, dim)], 1
    )
    q_own = queries.reshape(requests, tokens * heads, dim)
    v_par = swapped(v_own, "core")
    q_other = swapped(q_own, "y")
    near = [swapped(q_own, "z", flip) for flip in (1, 3)]
    k_par = swapped(k_own, "core")
    n_par = swapped(n_own, "core")
    vt = prepare(cached_len, v_own, v_par)
    q_other, vt = lax.optimization_barrier((q_other, vt))
    next_to = [swapped(q_other, "z", flip) for flip in (1, 3)]
    q_both, near = lax.optimization_barrier((jnp.stack([q_own, q_other]), near))
    far = swapped(q_both, "z", 2)

    common = (cached_len, span_order)
    keys = (k_own, k_par, n_own, n_par, vt)
    blocks = {(0, 0): 0, (0, 1): 1, (1, 0): 2, (3, 0): 3, (1, 1): 4, (3, 1): 5}
    arrays = [q_own, q_other, *near, *next_to, far]

    def tile(r, a, b):
        def half(place):
            return place + ((6, place[1]) if place[0] == 2 else (blocks[place], None))

        return (r, half(a), half(b))

    here, by_own, by_other, last = (
        ((0, 0), (0, 1)),
        ((1, 0), (3, 0)),
        ((1, 1), (3, 1)),
        ((2, 0), (2, 1)),
    )
    plan = (
        ((0, here), (0, by_own), (1, here)),
        ((0, by_other), (0, last)),
        ((1, by_own), (1, by_other), (1, last)),
    )
    plan = [tuple(tile(r, *pair) for r, pair in call) for call in plan]
    partials = attend(plan[0], VMEM, *common, arrays[:4], *keys, [], ())
    groups = [
        [
            (((y ^ core) * 4 + (z ^ (2 * core))) * 2 + core) * 8 + kv
            for z in range(4)
            for y in range(2)
            for kv in range(8)
        ]
        for core in range(2)
    ]
    received = []
    for r in range(requests):
        done = tuple(half[:2] for tile in plan[0] if tile[0] == r for half in tile[1:])
        (parts,) = attend(plan[1 + r], VMEM if r == 0 else VMEM_ALL, *common, arrays, *keys, [partials[r]], done)
        sent = parts.reshape((64,) + parts.shape[3:])
        got = lax.all_to_all(
            sent, ("y", "z", "core", "kv"), 0, 0, axis_index_groups=groups, tiled=True
        )
        received.append(got.reshape((8, 8) + parts.shape[3:]))
    results = []
    for r in range(requests):
        results = combine(r, requests, received[r], results)
    attention, norm = results
    return attention.reshape(requests, tokens // 8, 8 * heads, dim), norm


def solution(mesh):
    split = Mesh(mesh.devices.reshape(2, 4, 2, 8), ("y", "z", "core", "kv"))
    ctx = ("y", "z", "core")
    placed = P(None, ctx, "kv", None)
    return jax.shard_map(
        on_device,
        mesh=split,
        in_specs=(placed,) * 5 + (P(), P()),
        out_specs=(
            P(None, ctx + ("kv",), None, None),
            P(None, ctx + ("kv",), None),
        ),
        check_vma=False,
    )
```
